512 devices in a mesh: batch: 8 (over z_lo, core), frame: 4 (over x), row: 16 (over z_hi, y).
Axes of the slice: x: 4, y: 4, z: 16 (z_hi: 4, z_lo: 4; z = z_hi * 4 + z_lo), core: 2. Of those that a mesh axis runs over, the one named last changes fastest.
Arguments:
- block_input: bfloat16 [8, 16, 128, 32, 128], P('batch', 'frame', 'row'), may hold values from -90 to 90
- gain_first: float32 [128], replicated, may hold values from 0.5 to 2
- conv_weight: bfloat16 [3, 3, 3, 128, 128], replicated, may hold values from -0.109375 to 0.109375
- gain_second: float32 [128], replicated, may hold values from 0.5 to 2
- out_weight: bfloat16 [128, 3], replicated, may hold values from -0.5 to 0.5
- disc_first: bfloat16 [1, 4, 4, 3, 64], replicated, may hold values from -0.875 to 0.875
- disc_second: bfloat16 [2, 4, 4, 64, 128], replicated, may hold values from -0.125 to 0.125
- score_grad: float32 [8, 8, 32, 8, 128], P('batch', 'frame', 'row'), may hold values from -800 to 800
Outputs:
- input_grad: bfloat16 [8, 16, 128, 32, 128], P('batch', 'frame', 'row')
- update: float32 [3, 3, 3, 128, 128], replicated
The draws below stay inside these ranges and needn't reach their ends.
All inputs are finite; a program needn't handle non-finite values.
Results may differ from the reference program's by a relative error of at most 0.022.
Values may be sent and summed in bfloat16 or wider, within the bound.
A program may use at most 64 MiB of HBM per device.

```python
import math
import jax
import jax.numpy as jnp
from jax import lax

CH = 128
GROUPS = 32
D1 = 64
D2 = 128
FRAMES = 16
COLS = 32
CLIPS = 8
HEIGHT = 128
N_FRAME = 4
N_ROW = 16


def draw_block_input(key, part):
    key = jax.random.fold_in(key, 7)
    keys = jax.random.split(key, 4)
    shape = (CLIPS, FRAMES, HEIGHT, COLS, CH)
    basis = jax.random.truncated_normal(keys[0], -4.0, 4.0, shape, jnp.float32)
    common = 0.5
    trend = 3.0
    row_place = (jnp.arange(HEIGHT, dtype=jnp.float32) / (HEIGHT - 1))[None, None, :, None, None]
    frame_place = (jnp.arange(FRAMES, dtype=jnp.float32) / (FRAMES - 1))[None, :, None, None, None]
    levels = jnp.exp(jnp.log(10.0) * jax.random.uniform(keys[1], (CLIPS, FRAMES, HEIGHT, 1, 1), jnp.float32))
    rising = trend ** (row_place + frame_place - 1.0)
    channel = jnp.exp(jnp.log(10.0) * jax.random.uniform(keys[2], (CH,), jnp.float32))
    offsets = jax.random.uniform(keys[3], (CH,), jnp.float32, -1.5, 1.5)
    values = (basis + common * offsets * (0.5 + row_place)) * levels * rising * channel / 40.0
    return values.astype(jnp.bfloat16)


def draw_score_grad(key, part):
    key = jax.random.fold_in(key, 11)
    shape = (CLIPS, FRAMES // 2, HEIGHT // 4, COLS // 4, D2)
    basis = jax.random.truncated_normal(key, -6.0, 6.0, shape, jnp.float32)
    frame_first = (jnp.arange(FRAMES // 2) < FRAMES // 2 // N_FRAME).astype(jnp.float32)[None, :, None, None, None]
    row_first = (jnp.arange(HEIGHT // 4) < HEIGHT // 4 // N_ROW).astype(jnp.float32)[None, None, :, None, None]
    boost = 1.0 + 7.0 * frame_first * row_first
    return (basis * 16.0 * boost).astype(jnp.float32)


def bell_draw(own_key, extent, deviation, limit, kind=jnp.bfloat16):
    return jnp.clip(deviation * jax.random.normal(own_key, extent, jnp.float32), -limit, limit).astype(kind)


def setup_inputs(seed: int = 0) -> dict:
    streams_of = jax.random.split(jax.random.key(seed), 9)
    return {
        "block_input": draw_block_input(jax.random.fold_in(streams_of[8], 71), 0),
        "gain_first": jnp.clip(jnp.exp(jax.random.uniform(streams_of[1], (CH,), jnp.float32, math.log(0.5), math.log(2.0))), 0.5, 2.0),
        "conv_weight": bell_draw(streams_of[2], (3, 3, 3, CH, CH), (27 * CH) ** -0.5, 0.109375),
        "gain_second": jnp.clip(jnp.exp(jax.random.uniform(streams_of[3], (CH,), jnp.float32, math.log(0.5), math.log(2.0))), 0.5, 2.0),
        "out_weight": bell_draw(streams_of[4], (CH, 3), CH ** -0.5, 0.5),
        "disc_first": bell_draw(streams_of[5], (1, 4, 4, 3, D1), 48 ** -0.5, 0.875),
        "disc_second": bell_draw(streams_of[6], (2, 4, 4, D1, D2), (32 * D1) ** -0.5, 0.125),
        "score_grad": draw_score_grad(jax.random.fold_in(streams_of[8], 71), 0),
    }


EPSILON = 1e-06

def silu_slope(values):
    logistic = jax.nn.sigmoid(values)
    return logistic * (1.0 + values * (1.0 - logistic))

def product(left, right):
    return jnp.dot(left.astype(jnp.float32), right.astype(jnp.float32), precision=lax.Precision.HIGHEST)

def group_norm(values):
    shaped = values.reshape(values.shape[:-1] + (GROUPS, CH // GROUPS))
    average = lax.optimization_barrier(jnp.mean(shaped, axis=(0, 1, 2, 4), keepdims=True))
    centred = shaped - average
    variance = lax.optimization_barrier(jnp.mean(centred * centred, axis=(0, 1, 2, 4), keepdims=True))
    inverse = lax.rsqrt(variance + EPSILON)
    normed = (centred * inverse).reshape(values.shape)
    return (normed, jnp.broadcast_to(inverse, shaped.shape).reshape(values.shape))

def norm_backward(act_grad, scaled, normed, inverse, gain):
    weighted = act_grad * silu_slope(scaled) * gain
    shaped = weighted.reshape(weighted.shape[:-1] + (GROUPS, CH // GROUPS))
    normed_groups = normed.reshape(shaped.shape)
    first_mean = lax.optimization_barrier(jnp.mean(shaped, axis=(0, 1, 2, 4), keepdims=True))
    second_mean = lax.optimization_barrier(jnp.mean(shaped * normed_groups, axis=(0, 1, 2, 4), keepdims=True))
    return (shaped - first_mean - normed_groups * second_mean).reshape(weighted.shape) * inverse

def pad_space(values):
    return jnp.pad(values, ((0, 0), (1, 1), (1, 1), (0, 0)))

def strided_conv(extended, weight, rows_out):
    time_taps = weight.shape[0]
    cols_out = (extended.shape[2] - 2) // 2
    summed = None
    for tap_t in range(time_taps):
        for tap_r in range(4):
            for tap_c in range(4):
                source = extended[tap_t::time_taps, tap_r:tap_r + 2 * rows_out:2, tap_c:tap_c + 2 * cols_out:2]
                product_term = product(source, weight[tap_t, tap_r, tap_c])
                summed = product_term if summed is None else summed + product_term
    return summed

def strided_back(extended, weight):
    time_taps = weight.shape[0]
    frame_count, row_ext, col_ext, _ = extended.shape
    rows_out = row_ext - 2
    cols_out = col_ext - 2
    per_time = []
    for tap_t in range(time_taps):
        phases = [[None, None], [None, None]]
        for tap_r in range(4):
            for tap_c in range(4):
                row_start = 1 if tap_r < 2 else 0
                column_start = 1 if tap_c < 2 else 0
                source = extended[:, row_start:row_start + rows_out + 1, column_start:column_start + cols_out + 1]
                product_term = product(source, weight[tap_t, tap_r, tap_c].T)
                current = phases[tap_r % 2][tap_c % 2]
                phases[tap_r % 2][tap_c % 2] = product_term if current is None else current + product_term
        upper = jnp.stack([phases[0][0], phases[0][1]], axis=3)
        lower = jnp.stack([phases[1][0], phases[1][1]], axis=3)
        grid = jnp.stack([upper, lower], axis=2)
        per_time.append(grid.reshape(frame_count, 2 * rows_out + 2, 2 * cols_out + 2, -1))
    joined = jnp.stack(per_time, axis=1)
    return joined.reshape((frame_count * time_taps,) + joined.shape[2:])

def causal_conv(extended, weight):
    summed = None
    for tap_t in range(3):
        for tap_r in range(3):
            for tap_c in range(3):
                source = extended[tap_t:tap_t + FRAMES, tap_r:tap_r + HEIGHT, tap_c:tap_c + COLS]
                product_term = product(source, weight[tap_t, tap_r, tap_c])
                summed = product_term if summed is None else summed + product_term
    return summed

def causal_conv_back(extended, weight):
    summed = None
    for tap_t in range(3):
        for tap_r in range(3):
            for tap_c in range(3):
                source = extended[2 - tap_t:2 - tap_t + FRAMES, 2 - tap_r:2 - tap_r + HEIGHT, 2 - tap_c:2 - tap_c + COLS]
                product_term = product(source, weight[tap_t, tap_r, tap_c].T)
                summed = product_term if summed is None else summed + product_term
    return summed

def causal_conv_weight(extended, grad):
    blocks = []
    for tap_t in range(3):
        for tap_r in range(3):
            for tap_c in range(3):
                source = extended[tap_t:tap_t + FRAMES, tap_r:tap_r + HEIGHT, tap_c:tap_c + COLS]
                blocks.append(lax.dot_general(source.astype(jnp.float32), grad.astype(jnp.float32), (((0, 1, 2), (0, 1, 2)), ((), ())), precision=lax.Precision.HIGHEST))
    return jnp.stack(blocks).reshape(3, 3, 3, CH, CH)

def reference(block_input, gain_first, conv_weight, gain_second, out_weight, disc_first, disc_second, score_grad):

    def clip_grads(inputs):
        clip_input, clip_score = inputs
        wide_in = clip_input.astype(jnp.float32)
        normed_first, inverse_first = group_norm(wide_in)
        scaled_first = normed_first * gain_first
        act_first = jax.nn.silu(scaled_first).astype(jnp.bfloat16)
        extended = jnp.pad(act_first, ((2, 0), (1, 1), (1, 1), (0, 0)))
        branch = causal_conv(extended, conv_weight)
        mixed = (wide_in + branch).astype(jnp.bfloat16)
        normed_second, inverse_second = group_norm(mixed.astype(jnp.float32))
        scaled_second = normed_second * gain_second
        act_second = jax.nn.silu(scaled_second).astype(jnp.bfloat16)
        image = product(act_second, out_weight).astype(jnp.bfloat16)
        first_pre = strided_conv(pad_space(image), disc_first, HEIGHT // 2)
        first_act = jax.nn.silu(first_pre).astype(jnp.bfloat16)
        second_pre = strided_conv(pad_space(first_act), disc_second, HEIGHT // 4)
        score_pre = (clip_score * silu_slope(second_pre)).astype(jnp.bfloat16)
        first_full = strided_back(pad_space(score_pre), disc_second)[:, 1:-1, 1:-1]
        first_grad = (first_full * silu_slope(first_pre)).astype(jnp.bfloat16)
        image_grad = strided_back(pad_space(first_grad), disc_first)[:, 1:-1, 1:-1].astype(jnp.bfloat16)
        act_grad = product(image_grad, out_weight.T)
        mixed_grad = norm_backward(act_grad, scaled_second, normed_second, inverse_second, gain_second)
        branch_grad = mixed_grad.astype(jnp.bfloat16)
        branch_ext = jnp.pad(branch_grad, ((0, 2), (1, 1), (1, 1), (0, 0)))
        act_first_grad = causal_conv_back(branch_ext, conv_weight)
        weight_grad = causal_conv_weight(extended, branch_grad)
        input_grad = (mixed_grad + norm_backward(act_first_grad, scaled_first, normed_first, inverse_first, gain_first)).astype(jnp.bfloat16)
        return (input_grad, weight_grad)
    input_grad, weight_grads = lax.map(clip_grads, (block_input, score_grad))
    weight_grad = lax.optimization_barrier(jnp.sum(weight_grads, axis=0))
    update = weight_grad * lax.rsqrt(jnp.mean(weight_grad * weight_grad) + EPSILON)
    return (input_grad, update)
```

```python
import functools

import jax
import jax.numpy as jnp
from jax import lax
from jax.experimental import pallas as pl
from jax.experimental.pallas import tpu as pltpu
from jax.sharding import PartitionSpec as P

GROUPS = 32


EPSILON = 1e-06

def group_total(values):
    lane = lax.broadcasted_iota(jnp.int32, values.shape, 1)
    paired = values + jnp.where(
        lane % 2 == 0, pltpu.roll(values, 127, 1), pltpu.roll(values, 1, 1)
    )
    return paired + jnp.where(
        lane % 4 < 2, pltpu.roll(paired, 126, 1), pltpu.roll(paired, 2, 1)
    )


def place():
    batch = lax.axis_index("batch")
    row = lax.axis_index("row")
    return dict(
        batch=batch,
        z_lo=batch // 2,
        core=batch % 2,
        frame=lax.axis_index("frame"),
        row=row,
        z_hi=row // 4,
        y=row % 4,
    )


def device(me, **changed):
    at = dict(me, **changed)
    return (at["z_lo"] * 2 + at["core"], at["frame"], at["z_hi"] * 4 + at["y"])


def plane_peers(me):
    own = me["frame"] * 4 + me["y"]
    for step in range(1, 16):
        other = (own + step) % 16
        yield device(me, frame=other // 4, y=other % 4)


def high_peers(me):
    for step in range(1, 4):
        yield device(me, z_hi=(me["z_hi"] + step) % 4)


def broadcast_slot(buffer, slot, peers, send_sem, recv_sem):
    copies = []
    for peer in peers:
        copy = pltpu.make_async_remote_copy(
            src_ref=buffer.at[slot],
            dst_ref=buffer.at[slot],
            send_sem=send_sem,
            recv_sem=recv_sem,
            device_id=peer,
            device_id_type=pl.DeviceIdType.MESH,
        )
        copy.start()
        copies.append(copy)
    return copies


def wait_all(buffer, count, send_sem, recv_sem):
    whole = buffer.at[pl.ds(0, count)]
    pltpu.make_async_copy(whole, whole, recv_sem).wait()
    pltpu.make_async_copy(whole, whole, send_sem).wait()


def tile(row):
    return jnp.broadcast_to(row, (8, row.shape[-1]))


def enter(peers):
    barrier = pltpu.get_barrier_semaphore()
    for peer in peers:
        pl.semaphore_signal(
            barrier, inc=1, device_id=peer, device_id_type=pl.DeviceIdType.MESH
        )
    pl.semaphore_wait(barrier, len(peers))


def merged_moments(slots, entries):
    count = slots.shape[0]
    means, squares = (slots[:, 0, :], slots[:, 1, :])
    mean = group_total(tile(jnp.sum(means, axis=0, keepdims=True))) / (4 * count)
    apart = means - mean[0:1]
    total = jnp.sum(squares + entries * (apart * apart), axis=0, keepdims=True)
    return (mean, group_total(tile(total)))


def moments_kernel(entries, v_ref, o_ref, plane, high, send, recv):
    me = place()
    near, far = (list(plane_peers(me)), list(high_peers(me)))
    enter(near + far)
    slot = me["frame"] * 4 + me["y"]
    plane[slot] = v_ref[...]
    broadcast_slot(plane, slot, near, send.at[0], recv.at[0])
    wait_all(plane, 15, send.at[0], recv.at[0])
    mean, squares = merged_moments(plane[...], float(entries))
    high[me["z_hi"], 0:1, :] = mean[0:1]
    high[me["z_hi"], 1:2, :] = squares[0:1]
    broadcast_slot(high, me["z_hi"], far, send.at[1], recv.at[1])
    wait_all(high, 3, send.at[1], recv.at[1])
    means, squares = (high[:, 0, :], high[:, 1, :])
    mean = jnp.sum(means, axis=0, keepdims=True) / 4.0
    apart = means - mean
    total = jnp.sum(squares + (64.0 * entries) * (apart * apart), axis=0, keepdims=True)
    o_ref[0:1, :] = mean
    o_ref[1:2, :] = total / (256.0 * entries)


def sums_kernel(v_ref, o_ref, plane, high, send, recv):
    me = place()
    near, far = (list(plane_peers(me)), list(high_peers(me)))
    enter(near + far)
    slot = me["frame"] * 4 + me["y"]
    plane[slot] = v_ref[...]
    broadcast_slot(plane, slot, near, send.at[0], recv.at[0])
    wait_all(plane, 15, send.at[0], recv.at[0])
    sums = jnp.sum(plane[...], axis=0)
    high[me["z_hi"], 0:1, :] = group_total(tile(sums[0:1]))[0:1]
    high[me["z_hi"], 1:2, :] = group_total(tile(sums[1:2]))[0:1]
    broadcast_slot(high, me["z_hi"], far, send.at[1], recv.at[1])
    wait_all(high, 3, send.at[1], recv.at[1])
    o_ref[...] = jnp.sum(high[...], axis=0)


def clip_exchange(kernel, values, collective_id):
    lanes = values.shape[-1]
    return pl.pallas_call(
        kernel,
        out_shape=jax.ShapeDtypeStruct(values.shape, jnp.float32),
        in_specs=[pl.BlockSpec(memory_space=pltpu.VMEM)],
        out_specs=pl.BlockSpec(memory_space=pltpu.VMEM),
        scratch_shapes=[
            pltpu.VMEM((16, 2, lanes), jnp.float32),
            pltpu.VMEM((4, 2, lanes), jnp.float32),
            pltpu.SemaphoreType.DMA((2,)),
            pltpu.SemaphoreType.DMA((2,)),
        ],
        compiler_params=pltpu.CompilerParams(collective_id=collective_id, has_side_effects=True),
    )(values)


def z_peers(me):
    own = me["z_hi"] * 4 + me["z_lo"]
    for step in range(1, 16):
        other = (own + step) % 16
        yield device(me, z_hi=other // 4, z_lo=other % 4)


def update_kernel(
    w_ref, o_ref, pair_out, pair_in, x_out, x_in, y_out, y_in, z_out, z_in, z_all, gathered, send, recv
):
    me = place()
    core, frame, y, z = (me["core"], me["frame"], me["y"], me["z_hi"] * 4 + me["z_lo"])
    partner = [device(me, core=1 - core)]
    line = list(z_peers(me))
    x_others = [(frame + step) % 4 for step in range(1, 4)]
    y_others = [(y + step) % 4 for step in range(1, 4)]
    x_line = [device(me, frame=other) for other in x_others]
    y_line = [device(me, y=other) for other in y_others]
    enter(partner + x_line + y_line + line)

    def push(src, dst, peer, stage):
        pltpu.make_async_remote_copy(
            src_ref=src,
            dst_ref=dst,
            send_sem=send.at[stage],
            recv_sem=recv.at[stage],
            device_id=peer,
            device_id_type=pl.DeviceIdType.MESH,
        ).start()

    pair_out[...] = w_ref[1 - core].astype(jnp.bfloat16)
    push(pair_out, pair_in, partner[0], 0)
    wait_all(pair_out, 4, send.at[0], recv.at[0])
    x_out[...] = (w_ref[core] + pair_in[...].astype(jnp.float32)).astype(jnp.bfloat16)
    for other, peer in zip(x_others, x_line):
        push(x_out.at[other], x_in.at[frame], peer, 1)
    own = w_ref[core, frame] + pair_in[frame].astype(jnp.float32)
    x_in[frame] = jnp.zeros(x_in.shape[1:], x_in.dtype)
    wait_all(x_out, 3, send.at[1], recv.at[1])
    own = own + jnp.sum(x_in[...].astype(jnp.float32), axis=0)
    y_out[0:432, :] = own.astype(jnp.bfloat16)
    y_out[432:448, :] = jnp.zeros((16, 128), jnp.bfloat16)
    for other, peer in zip(y_others, y_line):
        push(y_out.at[pl.ds(other * 112, 112)], y_in.at[y], peer, 2)
    y_in[y] = y_out[pl.ds(y * 112, 112), :]
    wait_all(y_in, 3, send.at[2], recv.at[2])
    z_out[0:14] = jnp.sum(y_in[...].astype(jnp.float32), axis=0).reshape(14, 8, 128)
    z_out[14:16] = jnp.zeros((2, 8, 128), jnp.float32)
    for step, peer in enumerate(line):
        push(z_out.at[(z + 1 + step) % 16], z_in.at[z], peer, 3)
    z_in[z] = z_out[z]
    wait_all(z_in, 15, send.at[3], recv.at[3])
    z_all[z] = jnp.sum(z_in[...], axis=0)
    broadcast_slot(z_all, z, line, send.at[4], recv.at[4])
    wait_all(z_all, 15, send.at[4], recv.at[4])
    mine = gathered.at[core, frame]
    mine[y] = z_all[0:14].reshape(112, 128).astype(jnp.bfloat16)
    broadcast_slot(mine, y, y_line, send.at[5], recv.at[5])
    wait_all(mine, 3, send.at[5], recv.at[5])
    half = gathered.at[core]
    broadcast_slot(half, frame, x_line, send.at[6], recv.at[6])
    wait_all(half, 3, send.at[6], recv.at[6])
    broadcast_slot(gathered, core, partner, send.at[7], recv.at[7])
    wait_all(gathered, 1, send.at[7], recv.at[7])
    squares = jnp.zeros((8, 128), jnp.float32)
    for part in range(8):
        piece = gathered[part // 4, part % 4].reshape(448, 128)[0:432].astype(jnp.float32)
        squares = squares + jnp.sum((piece * piece).reshape(54, 8, 128), axis=0)
    mean = jnp.sum(squares, keepdims=True) / (8 * 432 * 128)
    scale = lax.rsqrt(mean + EPSILON)
    for part in range(8):
        piece = gathered[part // 4, part % 4].reshape(448, 128)[0:432].astype(jnp.float32)
        o_ref[part // 4, part % 4] = piece * scale


def summed_update(local_weight):
    low = jnp.bfloat16
    return pl.pallas_call(
        update_kernel,
        out_shape=jax.ShapeDtypeStruct((2, 4, 432, 128), jnp.float32),
        in_specs=[pl.BlockSpec(memory_space=pltpu.VMEM)],
        out_specs=pl.BlockSpec(memory_space=pltpu.VMEM),
        scratch_shapes=[
            pltpu.VMEM((4, 432, 128), low),
            pltpu.VMEM((4, 432, 128), low),
            pltpu.VMEM((4, 432, 128), low),
            pltpu.VMEM((4, 432, 128), low),
            pltpu.VMEM((448, 128), low),
            pltpu.VMEM((4, 112, 128), low),
            pltpu.VMEM((16, 8, 128), jnp.float32),
            pltpu.VMEM((16, 8, 128), jnp.float32),
            pltpu.VMEM((16, 8, 128), jnp.float32),
            pltpu.VMEM((2, 4, 4, 112, 128), low),
            pltpu.SemaphoreType.DMA((8,)),
            pltpu.SemaphoreType.DMA((8,)),
        ],
        compiler_params=pltpu.CompilerParams(
            collective_id=3, has_side_effects=True, vmem_limit_bytes=40 * 1024 * 1024
        ),
    )(local_weight.reshape(2, 4, 432, 128))


def with_halo(block, sides, width):
    for axis, dim in sides:
        count = lax.axis_size(axis)
        forward = [(i, i + 1) for i in range(count - 1)]
        backward = [(target, source) for source, target in forward]
        low = lax.ppermute(
            lax.slice_in_dim(block, block.shape[dim] - width, None, axis=dim), axis, forward
        )
        high = lax.ppermute(lax.slice_in_dim(block, 0, width, axis=dim), axis, backward)
        block = jnp.concatenate([low, block, high], axis=dim)
    return block


def passed_along(value, axis, steps):
    count = lax.axis_size(axis)
    leading, last = (max(0, -steps), min(count, count - steps))
    return lax.ppermute(value, axis, [(source, source + steps) for source in range(leading, last)])


def silu_slope(values):
    logistic = jax.nn.sigmoid(values)
    return logistic * (1.0 + values * (1.0 - logistic))


def norm_forward(values, groups, member_count):
    channels = values.shape[-1]
    entries = values.size // channels
    mean = jnp.mean(values, axis=(0, 1, 2))
    centred = values - mean
    squares = jnp.sum(centred * centred, axis=(0, 1, 2))
    kernel = functools.partial(moments_kernel, entries)
    mean, variance = clip_exchange(kernel, jnp.stack([mean, squares]), 1)
    inverse = lax.rsqrt(variance + EPSILON)
    return ((values - mean) * inverse, inverse)


def norm_backward(act_grad, scaled, normed, inverse, gain, groups, member_count):
    weighted = act_grad * silu_slope(scaled) * gain
    local = jnp.stack(
        [jnp.sum(weighted, axis=(0, 1, 2)), jnp.sum(weighted * normed, axis=(0, 1, 2))]
    )
    first_mean, second_mean = clip_exchange(sums_kernel, local, 2) / member_count
    return (weighted - first_mean - normed * second_mean) * inverse


def pad_columns(values):
    return jnp.pad(values, ((0, 0), (0, 0), (1, 1), (0, 0)))


def column_taps(window_slab, offsets, column_count):
    return jnp.concatenate(
        [
            lax.slice_in_dim(window_slab, offset, offset + column_count, axis=2)
            for offset in offsets
        ],
        axis=3,
    )


def causal_conv(extended, weight, frame_count, row_count, column_count):
    summed = None
    for tap_t in range(3):
        for tap_r in range(3):
            window_slab = extended[tap_t : tap_t + frame_count, tap_r : tap_r + row_count]
            stacked = column_taps(window_slab, (0, 1, 2), column_count)
            product_term = jnp.dot(
                stacked,
                weight[tap_t, tap_r].reshape(-1, weight.shape[-1]),
                preferred_element_type=jnp.float32,
            )
            summed = product_term if summed is None else summed + product_term
    return summed


def causal_conv_back(extended, weight, frame_count, row_count, column_count):
    flipped = jnp.swapaxes(weight, 3, 4)
    summed = None
    for tap_t in range(3):
        for tap_r in range(3):
            window_slab = extended[
                2 - tap_t : 2 - tap_t + frame_count, 2 - tap_r : 2 - tap_r + row_count
            ]
            stacked = column_taps(window_slab, (2, 1, 0), column_count)
            product_term = jnp.dot(
                stacked,
                flipped[tap_t, tap_r].reshape(-1, flipped.shape[-1]),
                preferred_element_type=jnp.float32,
            )
            summed = product_term if summed is None else summed + product_term
    return summed


def causal_conv_weight(extended, grad, frame_count, row_count, column_count):
    blocks = []
    for tap_t in range(3):
        for tap_r in range(3):
            window_slab = extended[tap_t : tap_t + frame_count, tap_r : tap_r + row_count]
            stacked = column_taps(window_slab, (0, 1, 2), column_count)
            blocks.append(
                lax.dot_general(
                    stacked,
                    grad,
                    (((0, 1, 2), (0, 1, 2)), ((), ())),
                    preferred_element_type=jnp.float32,
                )
            )
    channel_count = grad.shape[-1]
    return jnp.stack(blocks).reshape(3, 3, 3, channel_count, channel_count)


def strided_conv(extended, weight, rows_out):
    time_taps = weight.shape[0]
    cols_out = (extended.shape[2] - 2) // 2
    summed = None
    for tap_t in range(time_taps):
        for tap_r in range(4):
            for tap_c in range(4):
                source = extended[
                    tap_t::time_taps,
                    tap_r : tap_r + 2 * rows_out : 2,
                    tap_c : tap_c + 2 * cols_out : 2,
                ]
                product_term = jnp.dot(
                    source, weight[tap_t, tap_r, tap_c], preferred_element_type=jnp.float32
                )
                summed = product_term if summed is None else summed + product_term
    return summed


def strided_back(extended, weight):
    time_taps = weight.shape[0]
    frame_count, row_ext, col_ext, _ = extended.shape
    rows_out = row_ext - 2
    cols_out = col_ext - 2
    per_time = []
    for tap_t in range(time_taps):
        phases = [[None, None], [None, None]]
        for tap_r in range(4):
            for tap_c in range(4):
                row_start = 1 if tap_r < 2 else 0
                column_start = 1 if tap_c < 2 else 0
                source = extended[
                    :,
                    row_start : row_start + rows_out + 1,
                    column_start : column_start + cols_out + 1,
                ]
                product_term = jnp.dot(
                    source, weight[tap_t, tap_r, tap_c].T, preferred_element_type=jnp.float32
                )
                current = phases[tap_r % 2][tap_c % 2]
                phases[tap_r % 2][tap_c % 2] = (
                    product_term if current is None else current + product_term
                )
        upper = jnp.stack([phases[0][0], phases[0][1]], axis=3)
        lower = jnp.stack([phases[1][0], phases[1][1]], axis=3)
        grid = jnp.stack([upper, lower], axis=2)
        per_time.append(grid.reshape(frame_count, 2 * rows_out + 2, 2 * cols_out + 2, -1))
    joined = jnp.stack(per_time, axis=1)
    return joined.reshape((frame_count * time_taps,) + joined.shape[2:])


def shards(
    block_input,
    gain_first,
    conv_weight,
    gain_second,
    out_weight,
    disc_first,
    disc_second,
    score_grad,
):
    inputs = block_input[0]
    frame_count, row_count, column_count, channel_count = inputs.shape
    groups = GROUPS
    member_count = (
        frame_count
        * row_count
        * column_count
        * (channel_count // groups)
        * lax.axis_size("frame")
        * lax.axis_size("row")
    )
    wide_in = inputs.astype(jnp.float32)
    normed_first, inverse_first = norm_forward(wide_in, groups, member_count)
    scaled_first = normed_first * gain_first
    act_first = jax.nn.silu(scaled_first).astype(jnp.bfloat16)
    with_rows = with_halo(act_first, (("row", 1),), 1)
    earlier = passed_along(with_rows[frame_count - 2 :], "frame", 1)
    extended = pad_columns(jnp.concatenate([earlier, with_rows], axis=0))
    branch = causal_conv(extended, conv_weight, frame_count, row_count, column_count)
    mixed = (wide_in + branch).astype(jnp.bfloat16)
    normed_second, inverse_second = norm_forward(mixed.astype(jnp.float32), groups, member_count)
    scaled_second = normed_second * gain_second
    act_second = jax.nn.silu(scaled_second).astype(jnp.bfloat16)
    image = jnp.dot(act_second, out_weight, preferred_element_type=jnp.float32).astype(jnp.bfloat16)
    half_rows = row_count // 2
    image_ext = with_halo(image, (("row", 1),), 1)
    first_pre = strided_conv(pad_columns(image_ext), disc_first, half_rows)
    first_act = jax.nn.silu(first_pre).astype(jnp.bfloat16)
    first_ext = with_halo(first_act, (("row", 1),), 1)
    second_pre = strided_conv(pad_columns(first_ext), disc_second, row_count // 4)
    score_pre = (score_grad[0] * silu_slope(second_pre)).astype(jnp.bfloat16)
    score_ext = pad_columns(with_halo(score_pre, (("row", 1),), 1))
    first_full = strided_back(score_ext, disc_second)[:, :, 1:-1]
    first_grad = (first_full[:, 1:-1] * silu_slope(first_pre)).astype(jnp.bfloat16)
    feature_ext = with_halo(first_grad, (("row", 1),), 1)
    image_grad = strided_back(pad_columns(feature_ext), disc_first)[:, 1:-1, 1:-1].astype(
        jnp.bfloat16
    )
    act_grad = jnp.dot(image_grad, out_weight.T, preferred_element_type=jnp.float32)
    mixed_grad = norm_backward(
        act_grad, scaled_second, normed_second, inverse_second, gain_second, groups, member_count
    )
    branch_grad = mixed_grad.astype(jnp.bfloat16)
    grad_rows = with_halo(branch_grad, (("row", 1),), 1)
    later = passed_along(grad_rows[:2], "frame", -1)
    branch_ext = pad_columns(jnp.concatenate([grad_rows, later], axis=0))
    act_first_grad = causal_conv_back(branch_ext, conv_weight, frame_count, row_count, column_count)
    local_weight = causal_conv_weight(
        extended, branch_grad, frame_count, row_count, column_count
    ).reshape(-1)
    input_grad = (
        mixed_grad
        + norm_backward(
            act_first_grad,
            scaled_first,
            normed_first,
            inverse_first,
            gain_first,
            groups,
            member_count,
        )
    ).astype(jnp.bfloat16)
    update = summed_update(local_weight)
    return (input_grad[None], update.reshape(conv_weight.shape))


def solution(mesh):
    in_specs = (
        P("batch", "frame", "row", None, None),
        P(),
        P(),
        P(),
        P(),
        P(),
        P(),
        P("batch", "frame", "row", None, None),
    )
    out_specs = (P("batch", "frame", "row", None, None), P())
    return jax.shard_map(shards, mesh=mesh, in_specs=in_specs, out_specs=out_specs, check_vma=False)
```

```python
import jax
import jax.numpy as jnp
import numpy as np
from jax import lax
from jax.experimental import pallas as pl
from jax.experimental.pallas import tpu as pltpu
from jax.sharding import PartitionSpec as P

EPSILON = 1e-06
LOW = jnp.bfloat16
WIDE = jnp.float32
LOCAL = 1024
PER_CLIP = 64


def group_total(values):
    lane = lax.broadcasted_iota(jnp.int32, values.shape, 1)
    paired = values + jnp.where(
        lane % 2 == 0, pltpu.roll(values, 127, 1), pltpu.roll(values, 1, 1)
    )
    return paired + jnp.where(
        lane % 4 < 2, pltpu.roll(paired, 126, 1), pltpu.roll(paired, 2, 1)
    )


def tile(row):
    return jnp.broadcast_to(row, (8, row.shape[-1]))


def silu_slope(values):
    logistic = jax.nn.sigmoid(values)
    return logistic * (1.0 + values * (1.0 - logistic))


def place():
    batch = lax.axis_index("batch")
    row = lax.axis_index("row")
    return dict(
        batch=batch,
        z_lo=batch // 2,
        core=batch % 2,
        frame=lax.axis_index("frame"),
        row=row,
        z_hi=row // 4,
        y=row % 4,
    )


def device(me, **changed):
    at = dict(me, **changed)
    return (at["z_lo"] * 2 + at["core"], at["frame"], at["z_hi"] * 4 + at["y"])


def neighbour(me, frame_step, row_step):
    return (me["batch"], (me["frame"] + frame_step) % 4, (me["row"] + row_step) % 16)


def plane_peers(me):
    own = me["frame"] * 4 + me["y"]
    others = [(own + step) % 16 for step in range(1, 16)]
    return [(other, device(me, frame=other // 4, y=other % 4)) for other in others]


def z_peers(me):
    own = me["z_hi"] * 4 + me["z_lo"]
    others = [(own + step) % 16 for step in range(1, 16)]
    return [(other, device(me, z_hi=other // 4, z_lo=other % 4)) for other in others]


def high_peers(me):
    others = [(me["z_hi"] + step) % 4 for step in range(1, 4)]
    return [(other, device(me, z_hi=other)) for other in others]


def push(src, dst, peer, send_sem, recv_sem):
    pltpu.make_async_remote_copy(
        src_ref=src,
        dst_ref=dst,
        send_sem=send_sem,
        recv_sem=recv_sem,
        device_id=peer,
        device_id_type=pl.DeviceIdType.MESH,
    ).start()


def arrived(like, sem):
    pltpu.make_async_copy(like, like, sem).wait()


def selections():
    rows_first = np.zeros((160, 96), np.float32)
    for k in range(4):
        for a in range(10):
            for t in range(4):
                block, r = divmod(2 * a + k + 1, 8)
                rows_first[k * 40 + a * 4 + t, block * 32 + t * 8 + r] = 1
    rows_second = np.zeros((64, 40), np.float32)
    for m in range(2):
        for k in range(4):
            for u in range(2):
                for b in range(4):
                    rows_second[(m * 4 + k) * 8 + u * 4 + b, (2 * b + k) * 4 + 2 * u + m] = 1
    rows_back = np.zeros((32, 96), np.float32)
    for k in range(4):
        for a in range(2, 8):
            for t in range(4):
                r = 2 * a + k - 7
                if 0 <= r < 8:
                    rows_back[t * 8 + r, k * 24 + (a - 2) * 4 + t] = 1
    return (
        jnp.asarray(rows_first, LOW),
        jnp.asarray(rows_second, LOW),
        jnp.asarray(rows_second.T[8:32].copy(), WIDE),
        jnp.asarray(rows_back, WIDE),
    )


def column_sum(left, middle, right):
    column = lax.broadcasted_iota(jnp.int32, middle.shape, 0) % 32
    rows = middle.shape[0]
    return (
        middle
        + jnp.where(column == 0, 0.0, pltpu.roll(left, 1, 0))
        + jnp.where(column == 31, 0.0, pltpu.roll(right, rows - 1, 0))
    )


def across(left, right):
    return lax.dot_general(left, right, (((1,), (1,)), ((), ())), preferred_element_type=WIDE)


def wide_dot(left, right):
    return jnp.dot(left, right, preferred_element_type=WIDE)


def exact_pick(pick, values):
    return jnp.dot(pick, values, precision=lax.Precision.HIGHEST, preferred_element_type=WIDE)


def step_kernel(
    x_ref, gain1_ref, w_ref, gain2_ref, ow_ref, d1_ref, d2_ref, score_ref,
    pick_first, pick_second, pick_second_back, pick_first_back,
    out_ref, upd_ref,
    xe, ae, ge, mx, ag, wg, xt, g3, w_fwd, w_back,
    ow_f, ow_cols, ow_rows, d1_f, d1_rows, images, sg, sg_flat,
    dw, pair_out, pair_in, plane_out, plane_in, z_out, z_in, z_all, gathered,
    plane, high, stat_send, stat_recv, halo_send, halo_recv, sum_send, sum_recv,
):
    me = place()
    frame, row, core, y, z_hi = (me["frame"], me["row"], me["core"], me["y"], me["z_hi"])
    z = z_hi * 4 + me["z_lo"]
    slot = frame * 4 + y
    plane_line, z_line, high_line = (plane_peers(me), z_peers(me), high_peers(me))
    partner = device(me, core=1 - core)
    above, below = (neighbour(me, 0, -1), neighbour(me, 0, 1))
    corners = [neighbour(me, f, r) for f in (-1, 1) for r in (-1, 1)]

    barrier = pltpu.get_barrier_semaphore()
    greeted = [p for _, p in z_line] + [above, below] + corners
    greeted += [p for _, p in plane_line] + [partner]
    for peer in greeted:
        pl.semaphore_signal(
            barrier, inc=1, device_id=peer, device_id_type=pl.DeviceIdType.MESH
        )

    def plane_start(turn, first, second):
        plane[turn, slot, 0:1, :] = first
        plane[turn, slot, 1:2, :] = second
        for _, peer in plane_line:
            push(plane.at[turn, slot], plane.at[turn, slot], peer, stat_send.at[turn, 0], stat_recv.at[turn, 0])

    def plane_wait(turn):
        others = plane.at[turn, pl.ds(0, 15)]
        arrived(others, stat_recv.at[turn, 0])
        arrived(others, stat_send.at[turn, 0])

    def high_start(turn, first, second):
        high[turn, z_hi, 0:1, :] = first
        high[turn, z_hi, 1:2, :] = second
        for _, peer in high_line:
            push(high.at[turn, z_hi], high.at[turn, z_hi], peer, stat_send.at[turn, 1], stat_recv.at[turn, 1])

    def high_wait(turn):
        others = high.at[turn, pl.ds(0, 3)]
        arrived(others, stat_recv.at[turn, 1])
        arrived(others, stat_send.at[turn, 1])

    def moments_middle(turn):
        plane_wait(turn)
        means, squares = (plane[turn, :, 0, :], plane[turn, :, 1, :])
        mean = group_total(tile(jnp.sum(means, axis=0, keepdims=True))) / 64.0
        apart = means - mean[0:1]
        total = jnp.sum(squares + float(LOCAL) * (apart * apart), axis=0, keepdims=True)
        high_start(turn, mean[0:1], group_total(tile(total))[0:1])

    def moments_end(turn):
        high_wait(turn)
        means, squares = (high[turn, :, 0, :], high[turn, :, 1, :])
        mean = jnp.sum(means, axis=0, keepdims=True) / 4.0
        apart = means - mean
        total = jnp.sum(squares + (64.0 * LOCAL) * (apart * apart), axis=0, keepdims=True)
        return (mean, lax.rsqrt(total / (4.0 * LOCAL * PER_CLIP) + EPSILON))

    def sums_middle(turn):
        plane_wait(turn)
        sums = jnp.sum(plane[turn], axis=0)
        high_start(turn, group_total(tile(sums[0:1]))[0:1], group_total(tile(sums[1:2]))[0:1])

    def sums_end(turn):
        high_wait(turn)
        means = jnp.sum(high[turn], axis=0) / (4.0 * LOCAL * PER_CLIP)
        return (means[0:1], means[1:2])

    def local_moments(read):
        zero = jnp.zeros((1, 128), WIDE)
        total = lax.fori_loop(
            0, 4, lambda t, acc: acc + jnp.sum(read(t), axis=0, keepdims=True), zero
        )
        mean = total / float(LOCAL)

        def squares(t, acc):
            apart = read(t) - mean
            return acc + jnp.sum(apart * apart, axis=0, keepdims=True)

        return (mean, lax.fori_loop(0, 4, squares, zero))

    def halo_start(turn, src, dst, own_row, own_frames, to_frames, frame_step):
        def go(index, source, target, peer):
            push(source, target, peer, halo_send.at[turn, index], halo_recv.at[turn, index])

        inner = pl.ds(own_frames[0], 4)
        edge = pl.ds(own_frames[1], 2)
        base = pl.ds(own_frames[2], 4)
        far = pl.ds(to_frames, 2)
        go(0, src.at[inner, own_row + 7], dst.at[base, 0], below)
        go(1, src.at[inner, own_row], dst.at[base, 9], above)
        go(2, src.at[edge, pl.ds(own_row, 8)], dst.at[far, pl.ds(1, 8)], neighbour(me, frame_step, 0))
        go(3, src.at[edge, own_row + 7], dst.at[far, 0], neighbour(me, frame_step, 1))
        go(4, src.at[edge, own_row], dst.at[far, 9], neighbour(me, frame_step, -1))

    def halo_wait(turn, dst, base_frame, to_frames):
        base = pl.ds(base_frame, 4)
        far = pl.ds(to_frames, 2)
        parts = [
            dst.at[base, 0],
            dst.at[base, 9],
            dst.at[far, pl.ds(1, 8)],
            dst.at[far, 0],
            dst.at[far, 9],
        ]
        for index, part in enumerate(parts):
            arrived(part, halo_recv.at[turn, index])
            arrived(part, halo_send.at[turn, index])

    def inside(shape, outside_frame):
        position = lax.broadcasted_iota(jnp.int32, shape, 0)
        low = jnp.where(row == 0, 32, 0)
        high_end = jnp.where(row == 15, 288, 320)
        high_end = jnp.where(outside_frame, 0, high_end)
        return (position >= low) & (position < high_end)

    def own_input(t):
        return x_ref[t].astype(WIDE).reshape(256, 128)

    mean, squares = local_moments(own_input)
    xe[2:6, 1:9] = x_ref[...]
    sg[:, 1:3] = score_ref[...]
    pl.semaphore_wait(barrier, len(greeted))
    plane_start(0, mean, squares)
    halo_start(0, x_ref, xe, 0, (0, 2, 2), 0, 1)
    push(score_ref.at[:, 1], sg.at[:, 0], below, halo_send.at[0, 5], halo_recv.at[0, 5])
    push(score_ref.at[:, 0], sg.at[:, 3], above, halo_send.at[0, 6], halo_recv.at[0, 6])

    @pl.loop(0, 9)
    def _(tap):
        for c in range(3):
            w_fwd[pl.ds(tap * 128, 128), c * 128 : (c + 1) * 128] = w_ref[tap * 3 + c]

    moments_middle(0)

    ow_f[...] = jnp.zeros((128, 128), WIDE)
    ow_f[:, 0:3] = ow_ref[...].astype(WIDE)
    colours = ow_f[...]
    colours_t = colours.T
    for c in range(32):
        ow_cols[c * 128 : (c + 1) * 128, :] = (
            colours if c == 0 else pltpu.roll(colours, 3 * c, 1)
        ).astype(LOW)
        ow_rows[:, c * 128 : (c + 1) * 128] = (
            colours_t if c == 0 else pltpu.roll(colours_t, 3 * c, 0)
        ).astype(LOW)
    for k in range(4):
        d1_f[...] = jnp.zeros((128, 128), WIDE)
        for l in range(4):
            d1_f[3 * l : 3 * l + 3, 0:64] = d1_ref[k * 4 + l].astype(WIDE)
        single = d1_f[...]
        double = single + pltpu.roll(pltpu.roll(single, 64, 1), 6, 0)
        for p in range(8):
            d1_rows[k * 128 : (k + 1) * 128, p * 128 : (p + 1) * 128] = pltpu.roll(
                double, (12 * p - 3) % 128, 0
            ).astype(LOW)

    @pl.loop(0, 9)
    def _(tap):
        for c in range(3):
            w_back[pl.ds(tap * 128, 128), c * 128 : (c + 1) * 128] = (
                w_ref[tap * 3 + c].astype(WIDE).T.astype(LOW)
            )

    halo_wait(0, xe, 2, 0)
    for index in (5, 6):
        arrived(sg.at[:, 0], halo_recv.at[0, index])
        arrived(sg.at[:, 0], halo_send.at[0, index])
    gain1 = gain1_ref[...]
    gain2 = gain2_ref[...]
    mean1, inverse1 = moments_end(0)

    @pl.loop(0, 6)
    def _(t):
        scaled = (xe[t].astype(WIDE).reshape(320, 128) - mean1) * inverse1 * gain1
        act = scaled * jax.nn.sigmoid(scaled)
        keep = inside(act.shape, (t < 2) & (frame == 0))
        ae[t] = jnp.where(keep, act, 0.0).astype(LOW).reshape(10, 32, 128)

    @pl.loop(0, 4)
    def _(t):
        taps = [ae[t + i, j : j + 8].reshape(256, 128) for i in range(3) for j in range(3)]
        product = wide_dot(jnp.concatenate(taps, axis=1), w_fwd[...])
        branch = column_sum(product[:, 0:128], product[:, 128:256], product[:, 256:384])
        mx[t] = (xe[t + 2, 1:9].astype(WIDE).reshape(256, 128) + branch).astype(LOW)

    mean, squares = local_moments(lambda t: mx[t].astype(WIDE))
    plane_start(1, mean, squares)

    @pl.loop(0, 6)
    def _(t):
        for j in range(3):
            xt[j, t] = ae[t, j : j + 8].reshape(256, 128).astype(WIDE).T.astype(LOW)

    moments_middle(1)
    mean2, inverse2 = moments_end(1)

    def normed_second(t):
        return (mx[t].astype(WIDE) - mean2) * inverse2

    @pl.loop(0, 4)
    def _(t):
        scaled = normed_second(t) * gain2
        act = (scaled * jax.nn.sigmoid(scaled)).astype(LOW)
        ag[pl.ds(t * 256, 256), :] = act.astype(WIDE)

    image = jnp.zeros((32, 128), WIDE)
    for part in range(4):
        columns = [ag[pl.ds(c, 32, stride=32), :] for c in range(part * 8, part * 8 + 8)]
        image = image + wide_dot(
            jnp.concatenate(columns, axis=1).astype(LOW), ow_cols[part * 1024 : (part + 1) * 1024, :]
        )
    images[1] = image.astype(LOW)
    push(images.at[1], images.at[0], below, halo_send.at[1, 5], halo_recv.at[1, 5])
    push(images.at[1], images.at[2], above, halo_send.at[1, 6], halo_recv.at[1, 6])
    sg_flat[...] = sg[...].reshape(64, 128)
    score = jnp.concatenate([sg_flat[pl.ds(p, 8, stride=8), :] for p in range(8)], axis=0)
    for index in (5, 6):
        arrived(images.at[0], halo_recv.at[1, index])
        arrived(images.at[0], halo_send.at[1, index])

    strips = jnp.concatenate(
        [
            jnp.where(row == 0, 0.0, images[0].astype(WIDE)),
            images[1].astype(WIDE),
            jnp.where(row == 15, 0.0, images[2].astype(WIDE)),
        ],
        axis=0,
    ).astype(LOW)
    picked = wide_dot(pick_first[...], strips)
    taps = [picked[k * 40 : (k + 1) * 40] for k in range(4)]
    first_pre = wide_dot(jnp.concatenate(taps, axis=1).astype(LOW), d1_rows[...])
    place_row = lax.broadcasted_iota(jnp.int32, first_pre.shape, 0)
    low_row = jnp.where(row == 0, 12, 0)
    high_row = jnp.where(row == 15, 28, 40)
    real = (place_row >= low_row) & (place_row < high_row)
    first_act = jnp.where(real, first_pre * jax.nn.sigmoid(first_pre), 0.0).astype(LOW)
    picked = wide_dot(pick_second[...], first_act)
    blank = jnp.zeros((8, 128), WIDE)
    lane = lax.broadcasted_iota(jnp.int32, (64, 128), 1)
    second_pre = jnp.zeros((64, 128), WIDE)
    for tap in range(8):
        middle = jnp.concatenate(
            [picked[tap * 8 : tap * 8 + 8, p * 128 : (p + 1) * 128] for p in range(8)], axis=0
        )
        turned = pltpu.roll(middle, 64, 1)
        sides = jnp.where(
            lane < 64,
            jnp.concatenate([blank, turned[0:56]], axis=0),
            jnp.concatenate([turned[8:64], blank], axis=0),
        )
        weights = jnp.concatenate([d2_ref[tap * 4 + l] for l in (1, 2, 0, 3)], axis=0)
        second_pre = second_pre + wide_dot(
            jnp.concatenate([middle, sides], axis=1).astype(LOW), weights
        )
    strip = lax.broadcasted_iota(jnp.int32, (64, 128), 0) % 4
    first_strip = jnp.where(row == 0, 1, 0)
    last_strip = jnp.where(row == 15, 2, 3)
    score_pre = jnp.where(
        (strip >= first_strip) & (strip <= last_strip), score * silu_slope(second_pre), 0.0
    ).astype(LOW).astype(WIDE)
    sources = jnp.concatenate(
        [
            score_pre,
            jnp.concatenate([blank, score_pre[0:56]], axis=0),
            jnp.concatenate([score_pre[8:64], blank], axis=0),
        ],
        axis=1,
    ).astype(LOW)
    nothing = jnp.zeros((64, 128), LOW)
    spread = []
    for tap in range(8):
        even = jnp.concatenate([d2_ref[tap * 4 + 1], d2_ref[tap * 4 + 3], nothing], axis=1)
        odd = jnp.concatenate([d2_ref[tap * 4 + 2], nothing, d2_ref[tap * 4]], axis=1)
        back = across(sources, jnp.concatenate([even, odd], axis=0))
        spread.append(
            jnp.concatenate([back[p * 8 : (p + 1) * 8] for p in range(8)], axis=1)
        )
    first_full = exact_pick(pick_second_back[...], jnp.concatenate(spread, axis=0))
    first_grad = jnp.where(real[8:32], first_full * silu_slope(first_pre[8:32]), 0.0).astype(LOW)
    back = across(first_grad, d1_rows[...])
    stacked = jnp.concatenate([back[:, k * 128 : (k + 1) * 128] for k in range(4)], axis=0)
    image_grad = exact_pick(pick_first_back[...], stacked).astype(LOW)
    for part in range(4):
        grads = wide_dot(image_grad, ow_rows[:, part * 1024 : (part + 1) * 1024])
        for c in range(8):
            ag[pl.ds(part * 8 + c, 32, stride=32), :] = grads[:, c * 128 : (c + 1) * 128]

    def weigh(t, acc):
        normed = normed_second(t)
        here = pl.ds(t * 256, 256)
        weighted = ag[here, :] * silu_slope(normed * gain2) * gain2
        ag[here, :] = weighted
        return (
            acc[0] + jnp.sum(weighted, axis=0, keepdims=True),
            acc[1] + jnp.sum(weighted * normed, axis=0, keepdims=True),
        )

    zeros = (jnp.zeros((1, 128), WIDE), jnp.zeros((1, 128), WIDE))
    sums = lax.fori_loop(0, 4, weigh, zeros)
    plane_start(2, *sums)
    sums_middle(2)
    first_mean, second_mean = sums_end(2)

    @pl.loop(0, 4)
    def _(t):
        here = pl.ds(t * 256, 256)
        grad = (ag[here, :] - first_mean - normed_second(t) * second_mean) * inverse2
        ag[here, :] = grad
        low = grad.astype(LOW)
        ge[t, 1:9] = low.reshape(8, 32, 128)
        grad = low.astype(WIDE)
        column = lax.broadcasted_iota(jnp.int32, grad.shape, 0) % 32
        g3[here, 128:256] = low
        g3[here, 0:128] = jnp.where(column == 31, 0.0, pltpu.roll(grad, 255, 0)).astype(LOW)
        g3[here, 256:384] = jnp.where(column == 0, 0.0, pltpu.roll(grad, 1, 0)).astype(LOW)

    halo_start(1, ge, ge, 1, (0, 0, 0), 4, -1)

    for i in range(3):
        for j in range(3):
            acts = jnp.concatenate([xt[j, i + t] for t in range(4)], axis=1)
            product = wide_dot(acts, g3[...])
            for c in range(3):
                first = ((i * 3 + j) * 3 + c) * 128
                dw[first : first + 128, :] = product[:, c * 128 : (c + 1) * 128]
    dw[3456:3520, :] = jnp.zeros((64, 128), WIDE)
    theirs = pl.ds(pl.multiple_of((1 - core) * 1728, 64), 1792)
    ours = pl.ds(pl.multiple_of(core * 1728, 64), 1792)
    pair_out[...] = dw[theirs, :].astype(LOW)
    push(pair_out, pair_in, partner, sum_send.at[0], sum_recv.at[0])

    halo_wait(1, ge, 0, 4)

    def normed_first(t):
        return (own_input(t) - mean1) * inverse1

    def back_step(t, acc):
        taps = []
        for i in range(3):
            for j in range(3):
                strip = ge[t + 2 - i, 2 - j : 10 - j].reshape(256, 128)
                above_edge = (row == 0) if j == 2 else False
                below_edge = (row == 15) if j == 0 else False
                late = (frame == 3) & (t + 2 - i > 3)
                position = lax.broadcasted_iota(jnp.int32, (256, 128), 0)
                low = jnp.where(above_edge, 32, 0)
                end = jnp.where(late, 0, jnp.where(below_edge, 224, 256))
                keep = (position >= low) & (position < end)
                taps.append(jnp.where(keep, strip.astype(WIDE), 0.0).astype(LOW))
        product = wide_dot(jnp.concatenate(taps, axis=1), w_back[...])
        grad = column_sum(product[:, 256:384], product[:, 128:256], product[:, 0:128])
        normed = normed_first(t)
        weighted = grad * silu_slope(normed * gain1) * gain1
        wg[t] = weighted
        return (
            acc[0] + jnp.sum(weighted, axis=0, keepdims=True),
            acc[1] + jnp.sum(weighted * normed, axis=0, keepdims=True),
        )

    sums = lax.fori_loop(0, 4, back_step, zeros)
    plane_start(3, *sums)

    arrived(pair_in, sum_recv.at[0])
    arrived(pair_in, sum_send.at[0])
    plane_out[...] = (dw[ours, :] + pair_in[...].astype(WIDE)).astype(LOW).reshape(16, 112, 128)
    for other, peer in plane_line:
        push(plane_out.at[other], plane_in.at[slot], peer, sum_send.at[1], sum_recv.at[1])
    plane_in[slot] = plane_out[slot]

    sums_middle(3)

    arrived(plane_in.at[pl.ds(0, 15)], sum_recv.at[1])
    arrived(plane_in.at[pl.ds(0, 15)], sum_send.at[1])
    z_out[0:14] = jnp.sum(plane_in[...].astype(WIDE), axis=0).reshape(14, 8, 128)
    z_out[14:16] = jnp.zeros((2, 8, 128), WIDE)
    for other, peer in z_line:
        push(z_out.at[other], z_in.at[z], peer, sum_send.at[2], sum_recv.at[2])
    z_in[z] = z_out[z]

    first_mean, second_mean = sums_end(3)

    @pl.loop(0, 4)
    def _(t):
        grad = (wg[t] - first_mean - normed_first(t) * second_mean) * inverse1
        out_ref[t] = (ag[pl.ds(t * 256, 256), :] + grad).astype(LOW).reshape(8, 32, 128)

    arrived(z_in.at[pl.ds(0, 15)], sum_recv.at[2])
    arrived(z_in.at[pl.ds(0, 15)], sum_send.at[2])
    z_all[z] = jnp.sum(z_in[...], axis=0)
    for _, peer in z_line:
        push(z_all.at[z], z_all.at[z], peer, sum_send.at[3], sum_recv.at[3])
    arrived(z_all.at[pl.ds(0, 15)], sum_recv.at[3])
    arrived(z_all.at[pl.ds(0, 15)], sum_send.at[3])
    half = gathered.at[core]
    half[slot] = z_all[0:14].reshape(112, 128).astype(LOW)
    for _, peer in plane_line:
        push(half.at[slot], half.at[slot], peer, sum_send.at[4], sum_recv.at[4])
    arrived(half.at[pl.ds(0, 15)], sum_recv.at[4])
    arrived(half.at[pl.ds(0, 15)], sum_send.at[4])
    push(half, half, partner, sum_send.at[5], sum_recv.at[5])
    arrived(half, sum_recv.at[5])
    arrived(half, sum_send.at[5])

    def square(part, acc):
        for core_part in range(2):
            piece = gathered[core_part, part].astype(WIDE)
            piece = jnp.where(
                lax.broadcasted_iota(jnp.int32, piece.shape, 0) + part * 112 < 1728, piece, 0.0
            )
            acc = acc + jnp.sum((piece * piece).reshape(14, 8, 128), axis=0)
        return acc

    total = lax.fori_loop(0, 16, square, jnp.zeros((8, 128), WIDE))
    scale = lax.rsqrt(jnp.sum(total, keepdims=True) / (3456.0 * 128.0) + EPSILON)

    @pl.loop(0, 15)
    def _(part):
        for core_part in range(2):
            upd_ref[core_part, pl.ds(part * 112, 112), :] = gathered[core_part, part].astype(WIDE) * scale

    for core_part in range(2):
        upd_ref[core_part, 1680:1728, :] = gathered[core_part, 15, 0:48].astype(WIDE) * scale


def shards(
    block_input, gain_first, conv_weight, gain_second, out_weight, disc_first, disc_second, score_grad
):
    vmem = pl.BlockSpec(memory_space=pltpu.VMEM)
    low = lambda *shape: pltpu.VMEM(shape, LOW)
    wide = lambda *shape: pltpu.VMEM(shape, WIDE)
    dma = pltpu.SemaphoreType.DMA
    picks = selections()
    input_grad, update = pl.pallas_call(
        step_kernel,
        out_shape=(
            jax.ShapeDtypeStruct((4, 8, 32, 128), LOW),
            jax.ShapeDtypeStruct((2, 1728, 128), WIDE),
        ),
        in_specs=[vmem] * 12,
        out_specs=(vmem, vmem),
        scratch_shapes=[
            low(6, 10, 32, 128), low(6, 10, 32, 128), low(6, 10, 32, 128),
            low(4, 256, 128), wide(1024, 128), wide(4, 256, 128),
            low(3, 6, 128, 256), low(1024, 384), low(1152, 384), low(1152, 384),
            wide(128, 128), low(4096, 128), low(128, 4096), wide(128, 128), low(512, 1024),
            low(3, 32, 128), wide(2, 4, 8, 128), wide(64, 128),
            wide(3520, 128), low(1792, 128), low(1792, 128), low(16, 112, 128), low(16, 112, 128),
            wide(16, 8, 128), wide(16, 8, 128), wide(16, 8, 128), low(2, 16, 112, 128),
            wide(4, 16, 2, 128), wide(4, 4, 2, 128),
            dma((4, 2)), dma((4, 2)), dma((2, 7)), dma((2, 7)), dma((6,)), dma((6,)),
        ],
        compiler_params=pltpu.CompilerParams(
            collective_id=1, has_side_effects=True, vmem_limit_bytes=48 * 1024 * 1024
        ),
    )(
        block_input[0],
        gain_first.reshape(1, 128),
        conv_weight.reshape(27, 128, 128),
        gain_second.reshape(1, 128),
        out_weight,
        disc_first.reshape(16, 3, 64),
        disc_second.reshape(32, 64, 128),
        score_grad[0],
        *picks,
    )
    return (input_grad[None], update.reshape(conv_weight.shape))


def solution(mesh):
    split = P("batch", "frame", "row", None, None)
    in_specs = (split, P(), P(), P(), P(), P(), P(), split)
    return jax.shard_map(
        shards, mesh=mesh, in_specs=in_specs, out_specs=(split, P()), check_vma=False
    )
```

```python
import jax
import jax.numpy as jnp
import numpy as np
from jax import lax
from jax.experimental import pallas as pl
from jax.experimental.pallas import tpu as pltpu
from jax.sharding import PartitionSpec as P

EPSILON = 1e-06
LOW = jnp.bfloat16
WIDE = jnp.float32
LOCAL = 1024
PER_CLIP = 64


def group_total(values):
    lane = lax.broadcasted_iota(jnp.int32, values.shape, 1)
    paired = values + jnp.where(
        lane % 2 == 0, pltpu.roll(values, 127, 1), pltpu.roll(values, 1, 1)
    )
    return paired + jnp.where(
        lane % 4 < 2, pltpu.roll(paired, 126, 1), pltpu.roll(paired, 2, 1)
    )


def tile(row):
    return jnp.broadcast_to(row, (8, row.shape[-1]))


def silu_slope(values):
    logistic = jax.nn.sigmoid(values)
    return logistic * (1.0 + values * (1.0 - logistic))


def place():
    batch = lax.axis_index("batch")
    row = lax.axis_index("row")
    return dict(
        batch=batch,
        z_lo=batch // 2,
        core=batch % 2,
        frame=lax.axis_index("frame"),
        row=row,
        z_hi=row // 4,
        y=row % 4,
    )


def device(me, **changed):
    at = dict(me, **changed)
    return (at["z_lo"] * 2 + at["core"], at["frame"], at["z_hi"] * 4 + at["y"])


def neighbour(me, frame_step, row_step):
    return (me["batch"], (me["frame"] + frame_step) % 4, (me["row"] + row_step) % 16)


def plane_peers(me):
    own = me["frame"] * 4 + me["y"]
    others = [(own + step) % 16 for step in range(1, 16)]
    return [(other, device(me, frame=other // 4, y=other % 4)) for other in others]


def z_peers(me):
    own = me["z_hi"] * 4 + me["z_lo"]
    others = [(own + step) % 16 for step in range(1, 16)]
    return [(other, device(me, z_hi=other // 4, z_lo=other % 4)) for other in others]


def clip_peers(me):
    return [
        device(
            me,
            z_hi=(me["z_hi"] + dz) % 4,
            y=(me["y"] + dy) % 4,
            frame=(me["frame"] + dx) % 4,
        )
        for dz in (2, 1, 3, 0)
        for dy in (2, 1, 3, 0)
        for dx in (2, 1, 3, 0)
        if (dz, dy, dx) != (0, 0, 0)
    ]


def high_peers(me):
    others = [(me["z_hi"] + step) % 4 for step in range(1, 4)]
    return [(other, device(me, z_hi=other)) for other in others]


def push(src, dst, peer, send_sem, recv_sem):
    pltpu.make_async_remote_copy(
        src_ref=src,
        dst_ref=dst,
        send_sem=send_sem,
        recv_sem=recv_sem,
        device_id=peer,
        device_id_type=pl.DeviceIdType.MESH,
    ).start()


def arrived(like, sem):
    pltpu.make_async_copy(like, like, sem).wait()


def selections():
    rows_first = np.zeros((160, 96), np.float32)
    for k in range(4):
        for a in range(10):
            for t in range(4):
                block, r = divmod(2 * a + k + 1, 8)
                rows_first[k * 40 + a * 4 + t, block * 32 + t * 8 + r] = 1
    rows_second = np.zeros((64, 40), np.float32)
    for m in range(2):
        for k in range(4):
            for u in range(2):
                for b in range(4):
                    rows_second[(m * 4 + k) * 8 + u * 4 + b, (2 * b + k) * 4 + 2 * u + m] = 1
    rows_back = np.zeros((32, 96), np.float32)
    for k in range(4):
        for a in range(2, 8):
            for t in range(4):
                r = 2 * a + k - 7
                if 0 <= r < 8:
                    rows_back[t * 8 + r, k * 24 + (a - 2) * 4 + t] = 1
    return (
        jnp.asarray(rows_first, LOW),
        jnp.asarray(rows_second, LOW),
        jnp.asarray(rows_second.T[8:32].copy(), WIDE),
        jnp.asarray(rows_back, WIDE),
    )


def column_sum(left, middle, right):
    column = lax.broadcasted_iota(jnp.int32, middle.shape, 0) % 32
    rows = middle.shape[0]
    return (
        middle
        + jnp.where(column == 0, 0.0, pltpu.roll(left, 1, 0))
        + jnp.where(column == 31, 0.0, pltpu.roll(right, rows - 1, 0))
    )


def across(left, right):
    return lax.dot_general(left, right, (((1,), (1,)), ((), ())), preferred_element_type=WIDE)


def wide_dot(left, right):
    return jnp.dot(left, right, preferred_element_type=WIDE)


def exact_pick(pick, values):
    return jnp.dot(pick, values, precision=lax.Precision.HIGHEST, preferred_element_type=WIDE)


def step_kernel(
    x_hbm, gain1_hbm, w_hbm, gain2_hbm, ow_hbm, d1_hbm, d2_hbm, score_hbm,
    pick_first_hbm, pick_second_hbm, pick_second_back_hbm, pick_first_back_hbm,
    out_ref, summed_ref, scale_ref,
    gain1_ref, w_ref, gain2_ref, ow_ref, d1_ref, d2_ref,
    pick_first, pick_second, pick_second_back, pick_first_back,
    xe, ae, ge, mx, ag, wg, xt, g3, w_fwd, w_back,
    ow_f, ow_cols, ow_rows, d1_f, d1_rows, images, sg, sg_flat,
    dw, p1, reach, pair_out, pair_in, plane_out, plane_in, z_out, z_in, z_all, gathered,
    stats, plane, high, load_sem,
    stat_send, stat_recv, halo_send, halo_recv, sum_send, sum_recv,
):
    me = place()
    frame, row, core, y, z_hi = (me["frame"], me["row"], me["core"], me["y"], me["z_hi"])
    z = z_hi * 4 + me["z_lo"]
    slot = frame * 4 + y
    clip_slot = row * 4 + frame
    clip_line = clip_peers(me)
    plane_line, z_line, high_line = (plane_peers(me), z_peers(me), high_peers(me))
    partner = device(me, core=1 - core)
    above, below = (neighbour(me, 0, -1), neighbour(me, 0, 1))

    barrier = pltpu.get_barrier_semaphore()
    greeted = clip_line + [partner] + [
        device(me, z_hi=(z_hi + dz) % 4, z_lo=(me["z_lo"] + dl) % 4)
        for dz in range(4)
        for dl in range(1, 4)
    ]
    for peer in greeted:
        pl.semaphore_signal(
            barrier, inc=1, device_id=peer, device_id_type=pl.DeviceIdType.MESH
        )

    own_strip = (pl.ds(2, 4), pl.ds(1, 8))
    loads = [
        (x_hbm, xe.at[own_strip]),
        (score_hbm, sg.at[:, pl.ds(1, 2)]),
        (w_hbm, w_ref),
        (ow_hbm, ow_ref),
        (d1_hbm, d1_ref),
        (gain1_hbm, gain1_ref),
        (gain2_hbm, gain2_ref),
        (d2_hbm, d2_ref),
        (pick_first_hbm, pick_first),
        (pick_second_hbm, pick_second),
        (pick_second_back_hbm, pick_second_back),
        (pick_first_back_hbm, pick_first_back),
    ]
    loads = [
        pltpu.make_async_copy(src, dst, load_sem.at[index])
        for index, (src, dst) in enumerate(loads)
    ]
    for load in loads:
        load.start()

    def stats_start(turn, first, second):
        stats[turn, clip_slot, 0:1, :] = first
        stats[turn, clip_slot, 1:2, :] = second
        mine = stats.at[turn, clip_slot]
        for peer in clip_line:
            push(mine, mine, peer, stat_send.at[turn], stat_recv.at[turn])

    def stats_wait(turn):
        others = stats.at[turn, pl.ds(0, 63)]
        arrived(others, stat_recv.at[turn])
        arrived(others, stat_send.at[turn])

    def moments_end(turn):
        stats_wait(turn)
        parts = stats[turn]
        sums = jnp.sum(parts, axis=0)
        mean = group_total(tile(sums[0:1])) / (4.0 * PER_CLIP)
        apart = parts - mean[0:2]
        spread = jnp.sum(apart * apart, axis=0)
        total = group_total(tile(sums[1:2] + float(LOCAL) * spread[0:1]))
        return (mean[0:1], lax.rsqrt(total[0:1] / (4.0 * LOCAL * PER_CLIP) + EPSILON))

    def sums_end(turn):
        stats_wait(turn)
        sums = jnp.sum(stats[turn], axis=0) / (4.0 * LOCAL * PER_CLIP)
        return (group_total(tile(sums[0:1]))[0:1], group_total(tile(sums[1:2]))[0:1])

    def plane_start(first, second):
        plane[slot, 0:1, :] = first
        plane[slot, 1:2, :] = second
        for _, peer in plane_line:
            push(plane.at[slot], plane.at[slot], peer, stat_send.at[3], stat_recv.at[3])

    def plane_to_high():
        others = plane.at[pl.ds(0, 15)]
        arrived(others, stat_recv.at[3])
        arrived(others, stat_send.at[3])
        high[z_hi] = jnp.sum(plane[...], axis=0)
        for _, peer in high_line:
            push(high.at[z_hi], high.at[z_hi], peer, stat_send.at[4], stat_recv.at[4])

    def high_end():
        others = high.at[pl.ds(0, 3)]
        arrived(others, stat_recv.at[4])
        arrived(others, stat_send.at[4])
        sums = jnp.sum(high[...], axis=0) / (4.0 * LOCAL * PER_CLIP)
        return (group_total(tile(sums[0:1]))[0:1], group_total(tile(sums[1:2]))[0:1])

    def local_moments(read):
        zero = jnp.zeros((1, 128), WIDE)
        total = lax.fori_loop(
            0, 4, lambda t, acc: acc + jnp.sum(read(t), axis=0, keepdims=True), zero
        )
        mean = total / float(LOCAL)

        def squares(t, acc):
            apart = read(t) - mean
            return acc + jnp.sum(apart * apart, axis=0, keepdims=True)

        return (mean, lax.fori_loop(0, 4, squares, zero))

    def column_copies(t, values):
        here = pl.ds(t * 256, 256)
        values = values.astype(LOW)
        wide = values.astype(WIDE)
        column = lax.broadcasted_iota(jnp.int32, wide.shape, 0) % 32
        g3[here, 128:256] = values
        g3[here, 0:128] = jnp.where(column == 31, 0.0, pltpu.roll(wide, 255, 0)).astype(LOW)
        g3[here, 256:384] = jnp.where(column == 0, 0.0, pltpu.roll(wide, 1, 0)).astype(LOW)

    def acts_window(i, j):
        return jnp.concatenate([xt[j, i + t] for t in range(4)], axis=1)

    def against_acts(result):
        for i in range(3):
            for j in range(3):
                product = wide_dot(acts_window(i, j), g3[...])
                for c in range(3):
                    first = ((i * 3 + j) * 3 + c) * 128
                    result[first : first + 128, :] = product[:, c * 128 : (c + 1) * 128]

    def halo_start(turn, src, dst, own_row, own_frames, to_frames, frame_step):
        def go(index, source, target, peer):
            push(source, target, peer, halo_send.at[turn, index], halo_recv.at[turn, index])

        inner = pl.ds(own_frames[0], 4)
        edge = pl.ds(own_frames[1], 2)
        base = pl.ds(own_frames[2], 4)
        far = pl.ds(to_frames, 2)
        go(0, src.at[inner, own_row + 7], dst.at[base, 0], below)
        go(1, src.at[inner, own_row], dst.at[base, 9], above)
        go(2, src.at[edge, pl.ds(own_row, 8)], dst.at[far, pl.ds(1, 8)], neighbour(me, frame_step, 0))
        go(3, src.at[edge, own_row + 7], dst.at[far, 0], neighbour(me, frame_step, 1))
        go(4, src.at[edge, own_row], dst.at[far, 9], neighbour(me, frame_step, -1))

    def halo_wait(turn, dst, base_frame, to_frames):
        base = pl.ds(base_frame, 4)
        far = pl.ds(to_frames, 2)
        parts = [
            dst.at[base, 0],
            dst.at[base, 9],
            dst.at[far, pl.ds(1, 8)],
            dst.at[far, 0],
            dst.at[far, 9],
        ]
        for index, part in enumerate(parts):
            arrived(part, halo_recv.at[turn, index])
            arrived(part, halo_send.at[turn, index])

    def inside(shape, outside_frame):
        position = lax.broadcasted_iota(jnp.int32, shape, 0)
        low = jnp.where(row == 0, 32, 0)
        high_end = jnp.where(row == 15, 288, 320)
        high_end = jnp.where(outside_frame, 0, high_end)
        return (position >= low) & (position < high_end)

    def own_input(t):
        return xe[t + 2, 1:9].astype(WIDE).reshape(256, 128)

    loads[0].wait()
    mean, squares = local_moments(own_input)
    loads[1].wait()
    pl.semaphore_wait(barrier, len(greeted))
    stats_start(0, mean, squares)
    halo_start(0, xe, xe, 1, (2, 4, 2), 0, 1)
    push(sg.at[:, 2], sg.at[:, 0], below, halo_send.at[0, 5], halo_recv.at[0, 5])
    push(sg.at[:, 1], sg.at[:, 3], above, halo_send.at[0, 6], halo_recv.at[0, 6])
    for load in loads[2:]:
        load.wait()

    @pl.loop(0, 9)
    def _(tap):
        for c in range(3):
            w_fwd[pl.ds(tap * 128, 128), c * 128 : (c + 1) * 128] = w_ref[tap * 3 + c]

    ow_f[...] = jnp.zeros((128, 128), WIDE)
    ow_f[0:3, :] = ow_ref[...].astype(WIDE)
    colours_t = ow_f[...]
    colours = colours_t.T
    for c in range(32):
        ow_cols[c * 128 : (c + 1) * 128, :] = (
            colours if c == 0 else pltpu.roll(colours, 3 * c, 1)
        ).astype(LOW)
        ow_rows[:, c * 128 : (c + 1) * 128] = (
            colours_t if c == 0 else pltpu.roll(colours_t, 3 * c, 0)
        ).astype(LOW)
    for k in range(4):
        d1_f[...] = jnp.zeros((128, 128), WIDE)
        for colour in range(3):
            taps = d1_ref[k * 3 + colour].astype(WIDE)
            for l in range(4):
                d1_f[3 * l + colour : 3 * l + colour + 1, 0:64] = taps[l : l + 1]
        single = d1_f[...]
        double = single + pltpu.roll(pltpu.roll(single, 64, 1), 6, 0)
        for p in range(8):
            d1_rows[k * 128 : (k + 1) * 128, p * 128 : (p + 1) * 128] = pltpu.roll(
                double, (12 * p - 3) % 128, 0
            ).astype(LOW)

    @pl.loop(0, 9)
    def _(tap):
        for c in range(3):
            w_back[pl.ds(tap * 128, 128), c * 128 : (c + 1) * 128] = (
                w_ref[tap * 3 + c].astype(WIDE).T.astype(LOW)
            )

    halo_wait(0, xe, 2, 0)
    for index in (5, 6):
        arrived(sg.at[:, 0], halo_recv.at[0, index])
        arrived(sg.at[:, 0], halo_send.at[0, index])
    gain1 = gain1_ref[...]
    gain2 = gain2_ref[...]
    mean1, inverse1 = moments_end(0)

    @pl.loop(0, 6)
    def _(t):
        scaled = (xe[t].astype(WIDE).reshape(320, 128) - mean1) * inverse1 * gain1
        act = scaled * jax.nn.sigmoid(scaled)
        keep = inside(act.shape, (t < 2) & (frame == 0))
        ae[t] = jnp.where(keep, act, 0.0).astype(LOW).reshape(10, 32, 128)

    @pl.loop(0, 4)
    def _(t):
        taps = [ae[t + i, j : j + 8].reshape(256, 128) for i in range(3) for j in range(3)]
        product = wide_dot(jnp.concatenate(taps, axis=1), w_fwd[...])
        branch = column_sum(product[:, 0:128], product[:, 128:256], product[:, 256:384])
        mx[t] = (xe[t + 2, 1:9].astype(WIDE).reshape(256, 128) + branch).astype(LOW)

    mean, squares = local_moments(lambda t: mx[t].astype(WIDE))
    stats_start(1, mean, squares)

    @pl.loop(0, 6)
    def _(t):
        for j in range(3):
            xt[j, t] = ae[t, j : j + 8].reshape(256, 128).astype(WIDE).T.astype(LOW)

    column = lax.broadcasted_iota(jnp.int32, (1024, 128), 0) % 32
    tap_lane = lax.broadcasted_iota(jnp.int32, (1024, 128), 1)
    reached = ((tap_lane != 0) | (column < 31)) & ((tap_lane != 2) | (column > 0))
    reached = jnp.where(reached, 1.0, 0.0).astype(LOW)
    for i in range(3):
        for j in range(3):
            reach[i * 3 + j] = wide_dot(acts_window(i, j), reached)

    mean2, inverse2 = moments_end(1)

    def normed_second(t):
        return (mx[t].astype(WIDE) - mean2) * inverse2

    @pl.loop(0, 4)
    def _(t):
        scaled = normed_second(t) * gain2
        act = (scaled * jax.nn.sigmoid(scaled)).astype(LOW)
        ag[pl.ds(t * 256, 256), :] = act.astype(WIDE)

    image = jnp.zeros((32, 128), WIDE)
    for part in range(4):
        columns = [ag[pl.ds(c, 32, stride=32), :] for c in range(part * 8, part * 8 + 8)]
        image = image + wide_dot(
            jnp.concatenate(columns, axis=1).astype(LOW), ow_cols[part * 1024 : (part + 1) * 1024, :]
        )
    images[1] = image.astype(LOW)
    push(images.at[1], images.at[0], below, halo_send.at[1, 5], halo_recv.at[1, 5])
    push(images.at[1], images.at[2], above, halo_send.at[1, 6], halo_recv.at[1, 6])

    @pl.loop(0, 4)
    def _(t):
        column_copies(t, normed_second(t))

    against_acts(p1)
    sg_flat[...] = sg[...].reshape(64, 128)
    score = jnp.concatenate([sg_flat[pl.ds(p, 8, stride=8), :] for p in range(8)], axis=0)
    for index in (5, 6):
        arrived(images.at[0], halo_recv.at[1, index])
        arrived(images.at[0], halo_send.at[1, index])

    strips = jnp.concatenate(
        [
            jnp.where(row == 0, 0.0, images[0].astype(WIDE)),
            images[1].astype(WIDE),
            jnp.where(row == 15, 0.0, images[2].astype(WIDE)),
        ],
        axis=0,
    ).astype(LOW)
    picked = wide_dot(pick_first[...], strips)
    taps = [picked[k * 40 : (k + 1) * 40] for k in range(4)]
    first_pre = wide_dot(jnp.concatenate(taps, axis=1).astype(LOW), d1_rows[...])
    place_row = lax.broadcasted_iota(jnp.int32, first_pre.shape, 0)
    low_row = jnp.where(row == 0, 12, 0)
    high_row = jnp.where(row == 15, 28, 40)
    real = (place_row >= low_row) & (place_row < high_row)
    first_act = jnp.where(real, first_pre * jax.nn.sigmoid(first_pre), 0.0).astype(LOW)
    picked = wide_dot(pick_second[...], first_act)
    blank = jnp.zeros((8, 128), WIDE)
    lane = lax.broadcasted_iota(jnp.int32, (64, 128), 1)
    second_pre = jnp.zeros((64, 128), WIDE)
    for tap in range(8):
        middle = jnp.concatenate(
            [picked[tap * 8 : tap * 8 + 8, p * 128 : (p + 1) * 128] for p in range(8)], axis=0
        )
        turned = pltpu.roll(middle, 64, 1)
        sides = jnp.where(
            lane < 64,
            jnp.concatenate([blank, turned[0:56]], axis=0),
            jnp.concatenate([turned[8:64], blank], axis=0),
        )
        weights = jnp.concatenate([d2_ref[tap * 4 + l] for l in (1, 2, 0, 3)], axis=0)
        second_pre = second_pre + wide_dot(
            jnp.concatenate([middle, sides], axis=1).astype(LOW), weights
        )
    strip = lax.broadcasted_iota(jnp.int32, (64, 128), 0) % 4
    first_strip = jnp.where(row == 0, 1, 0)
    last_strip = jnp.where(row == 15, 2, 3)
    score_pre = jnp.where(
        (strip >= first_strip) & (strip <= last_strip), score * silu_slope(second_pre), 0.0
    ).astype(LOW).astype(WIDE)
    sources = jnp.concatenate(
        [
            score_pre,
            jnp.concatenate([blank, score_pre[0:56]], axis=0),
            jnp.concatenate([score_pre[8:64], blank], axis=0),
        ],
        axis=1,
    ).astype(LOW)
    nothing = jnp.zeros((64, 128), LOW)
    spread = []
    for tap in range(8):
        even = jnp.concatenate([d2_ref[tap * 4 + 1], d2_ref[tap * 4 + 3], nothing], axis=1)
        odd = jnp.concatenate([d2_ref[tap * 4 + 2], nothing, d2_ref[tap * 4]], axis=1)
        back = across(sources, jnp.concatenate([even, odd], axis=0))
        spread.append(
            jnp.concatenate([back[p * 8 : (p + 1) * 8] for p in range(8)], axis=1)
        )
    first_full = exact_pick(pick_second_back[...], jnp.concatenate(spread, axis=0))
    first_grad = jnp.where(real[8:32], first_full * silu_slope(first_pre[8:32]), 0.0).astype(LOW)
    back = across(first_grad, d1_rows[...])
    stacked = jnp.concatenate([back[:, k * 128 : (k + 1) * 128] for k in range(4)], axis=0)
    image_grad = exact_pick(pick_first_back[...], stacked).astype(LOW)
    for part in range(4):
        grads = wide_dot(image_grad, ow_rows[:, part * 1024 : (part + 1) * 1024])
        for c in range(8):
            ag[pl.ds(part * 8 + c, 32, stride=32), :] = grads[:, c * 128 : (c + 1) * 128]

    def weigh(t, acc):
        normed = normed_second(t)
        here = pl.ds(t * 256, 256)
        weighted = ag[here, :] * silu_slope(normed * gain2) * gain2
        ag[here, :] = weighted
        column_copies(t, weighted * inverse2)
        return (
            acc[0] + jnp.sum(weighted, axis=0, keepdims=True),
            acc[1] + jnp.sum(weighted * normed, axis=0, keepdims=True),
        )

    zeros = (jnp.zeros((1, 128), WIDE), jnp.zeros((1, 128), WIDE))
    sums = lax.fori_loop(0, 4, weigh, zeros)
    stats_start(2, *sums)
    against_acts(dw)
    first_mean, second_mean = sums_end(2)

    @pl.loop(0, 4)
    def _(t):
        here = pl.ds(t * 256, 256)
        grad = (ag[here, :] - first_mean - normed_second(t) * second_mean) * inverse2
        ag[here, :] = grad
        ge[t, 1:9] = grad.astype(LOW).reshape(8, 32, 128)

    halo_start(1, ge, ge, 1, (0, 0, 0), 4, -1)

    first_part, second_part = (first_mean * inverse2, second_mean * inverse2)
    for i in range(9):
        for c in range(3):
            rows = slice((i * 3 + c) * 128, (i * 3 + c) * 128 + 128)
            dw[rows, :] = (
                dw[rows, :] - reach[i, :, c : c + 1] * first_part - p1[rows, :] * second_part
            )
    dw[3456:3520, :] = jnp.zeros((64, 128), WIDE)
    theirs = pl.ds(pl.multiple_of((1 - core) * 1728, 64), 1792)
    ours = pl.ds(pl.multiple_of(core * 1728, 64), 1792)
    chunks = (pl.ds(0, 64), pl.ds(64, 48))
    pair_out[...] = dw[theirs, :].astype(LOW).reshape(16, 112, 128)
    for turn, chunk in enumerate(chunks):
        push(pair_out.at[:, chunk], pair_in.at[:, chunk], partner, sum_send.at[turn], sum_recv.at[turn])

    for turn, chunk in enumerate(chunks):
        arrived(pair_in.at[:, chunk], sum_recv.at[turn])
        arrived(pair_in.at[:, chunk], sum_send.at[turn])
        mine = dw[ours, :].reshape(16, 112, 128)[:, chunk.start : chunk.start + chunk.size]
        plane_out[:, chunk] = (mine + pair_in[:, chunk].astype(WIDE)).astype(LOW)
        for other, peer in plane_line:
            push(
                plane_out.at[other, chunk],
                plane_in.at[slot, chunk],
                peer,
                sum_send.at[2 + turn],
                sum_recv.at[2 + turn],
            )
        plane_in[slot, chunk] = plane_out[slot, chunk]

    tiles = (range(0, 4), range(4, 7))
    owns = (me["z_lo"] == 0, (me["z_lo"] == 2) & (z_hi < 3))
    for turn, chunk in enumerate(chunks):
        others = plane_in.at[pl.ds(0, 15), chunk]
        arrived(others, sum_recv.at[2 + turn])
        arrived(others, sum_send.at[2 + turn])
        total = jnp.sum(plane_in[:, chunk].astype(WIDE), axis=0).astype(LOW)
        for index, part in enumerate(tiles[turn]):
            z_out[part] = total[index * 16 : (index + 1) * 16]
            owner = (index, 2 * turn)

            @pl.when((z_hi != owner[0]) | (me["z_lo"] != owner[1]))
            def _():
                push(
                    z_out.at[part],
                    z_in.at[z],
                    device(me, z_hi=owner[0], z_lo=owner[1]),
                    sum_send.at[4 + turn],
                    sum_recv.at[4],
                )

    halo_wait(1, ge, 0, 4)

    def normed_first(t):
        return (own_input(t) - mean1) * inverse1

    def back_step(t, acc):
        taps = []
        for i in range(3):
            for j in range(3):
                strip = ge[t + 2 - i, 2 - j : 10 - j].reshape(256, 128)
                above_edge = (row == 0) if j == 2 else False
                below_edge = (row == 15) if j == 0 else False
                late = (frame == 3) & (t + 2 - i > 3)
                position = lax.broadcasted_iota(jnp.int32, (256, 128), 0)
                low = jnp.where(above_edge, 32, 0)
                end = jnp.where(late, 0, jnp.where(below_edge, 224, 256))
                keep = (position >= low) & (position < end)
                taps.append(jnp.where(keep, strip.astype(WIDE), 0.0).astype(LOW))
        product = wide_dot(jnp.concatenate(taps, axis=1), w_back[...])
        grad = column_sum(product[:, 256:384], product[:, 128:256], product[:, 0:128])
        normed = normed_first(t)
        weighted = grad * silu_slope(normed * gain1) * gain1
        wg[t] = weighted
        return (
            acc[0] + jnp.sum(weighted, axis=0, keepdims=True),
            acc[1] + jnp.sum(weighted * normed, axis=0, keepdims=True),
        )

    sums = lax.fori_loop(0, 4, back_step, zeros)
    plane_start(*sums)

    for turn in range(2):

        @pl.when(owns[turn])
        def _():
            part = z_hi + 4 * turn
            z_in[z] = z_out[part]
            arrived(z_in.at[pl.ds(0, 15)], sum_recv.at[4])
            z_all[part] = jnp.sum(z_in[...].astype(WIDE), axis=0).astype(LOW)
            for _, peer in z_line:
                push(z_all.at[part], z_all.at[part], peer, sum_send.at[6], sum_recv.at[6 + turn])

    plane_to_high()

    half, other_half = (gathered.at[core], gathered.at[1 - core])
    for turn, chunk in enumerate(chunks):
        count = len(tiles[turn])

        @pl.when(owns[turn])
        def _():
            arrived(z_all.at[pl.ds(0, count - 1)], sum_recv.at[6 + turn])
            arrived(z_out.at[pl.ds(0, count - 1)], sum_send.at[4 + turn])
            arrived(z_in.at[pl.ds(0, 15)], sum_send.at[6])

        @pl.when(jnp.logical_not(owns[turn]))
        def _():
            arrived(z_all.at[pl.ds(0, count)], sum_recv.at[6 + turn])
            arrived(z_out.at[pl.ds(0, count)], sum_send.at[4 + turn])

        first = tiles[turn].start
        half[slot, chunk] = z_all[first : first + count].reshape(count * 16, 128)
        for _, peer in plane_line:
            push(
                half.at[slot, chunk],
                half.at[slot, chunk],
                peer,
                sum_send.at[8 + turn],
                sum_recv.at[8 + turn],
            )

    first_mean, second_mean = high_end()

    @pl.loop(0, 4)
    def _(t):
        grad = (wg[t] - first_mean - normed_first(t) * second_mean) * inverse1
        out_ref[t] = (ag[pl.ds(t * 256, 256), :] + grad).astype(LOW).reshape(8, 32, 128)

    def squares_of(part_of, chunk):
        def add(part, acc):
            piece = part_of[part, chunk].astype(WIDE)
            return acc + jnp.sum((piece * piece).reshape(chunk.size // 8, 8, 128), axis=0)

        total = lax.fori_loop(0, 15, add, jnp.zeros((8, 128), WIDE))
        if chunk.start == 0:
            piece = part_of[15, 0:48].astype(WIDE)
            total = total + jnp.sum((piece * piece).reshape(6, 8, 128), axis=0)
        return total

    squares = []
    for turn, chunk in enumerate(chunks):
        others = half.at[pl.ds(0, 15), chunk]
        arrived(others, sum_recv.at[8 + turn])
        arrived(others, sum_send.at[8 + turn])
        push(half.at[:, chunk], half.at[:, chunk], partner, sum_send.at[10 + turn], sum_recv.at[10 + turn])
        squares.append(squares_of(half, chunk))
    for turn, chunk in enumerate(chunks):
        arrived(other_half.at[:, chunk], sum_recv.at[10 + turn])
        arrived(half.at[:, chunk], sum_send.at[10 + turn])
        squares.append(squares_of(other_half, chunk))
    total = (squares[0] + squares[1]) + (squares[2] + squares[3])
    mean = jnp.sum(total, keepdims=True) / (3456.0 * 128.0)
    scale_ref[...] = jnp.broadcast_to(lax.rsqrt(mean + EPSILON), (8, 128))
    summed_ref[...] = gathered[...]


def finish_kernel(grad_ref, summed_ref, scale_ref, out_ref, upd_ref):
    out_ref[...] = grad_ref[...]
    scale = scale_ref[0:1, :]
    for core in range(2):
        values = summed_ref[core, 0:15].reshape(1680, 128)
        upd_ref[core, 0:1680, :] = values.astype(WIDE) * scale
        upd_ref[core, 1680:1728, :] = summed_ref[core, 15, 0:48].astype(WIDE) * scale


def shards(
    block_input, gain_first, conv_weight, gain_second, out_weight, disc_first, disc_second, score_grad
):
    vmem = pl.BlockSpec(memory_space=pltpu.VMEM)
    low = lambda *shape: pltpu.VMEM(shape, LOW)
    wide = lambda *shape: pltpu.VMEM(shape, WIDE)
    dma = pltpu.SemaphoreType.DMA
    picks = selections()
    hbm = pl.BlockSpec(memory_space=pltpu.HBM)
    input_grad, summed, scale = pl.pallas_call(
        step_kernel,
        out_shape=(
            jax.ShapeDtypeStruct((4, 8, 32, 128), LOW),
            jax.ShapeDtypeStruct((2, 16, 112, 128), LOW),
            jax.ShapeDtypeStruct((8, 128), WIDE),
        ),
        in_specs=[hbm] * 12,
        out_specs=(vmem, vmem, vmem),
        scratch_shapes=[
            wide(1, 128), low(27, 128, 128), wide(1, 128), low(3, 128), low(12, 4, 64),
            low(32, 64, 128), low(160, 96), low(64, 40), wide(24, 64), wide(32, 96),
            low(6, 10, 32, 128), low(6, 10, 32, 128), low(6, 10, 32, 128),
            low(4, 256, 128), wide(1024, 128), wide(4, 256, 128),
            low(3, 6, 128, 256), low(1024, 384), low(1152, 384), low(1152, 384),
            wide(128, 128), low(4096, 128), low(128, 4096), wide(128, 128), low(512, 1024),
            low(3, 32, 128), wide(2, 4, 8, 128), wide(64, 128),
            wide(3520, 128), wide(3456, 128), wide(9, 128, 128), low(16, 112, 128), low(16, 112, 128), low(16, 112, 128), low(16, 112, 128),
            low(7, 16, 128), low(16, 16, 128), low(7, 16, 128), low(2, 16, 112, 128),
            wide(3, 64, 2, 128), wide(16, 2, 128), wide(4, 2, 128),
            dma((12,)), dma((5,)), dma((5,)), dma((2, 7)), dma((2, 7)), dma((12,)), dma((12,)),
        ],
        compiler_params=pltpu.CompilerParams(
            collective_id=1, has_side_effects=True, vmem_limit_bytes=64 * 1024 * 1024
        ),
    )(
        block_input[0],
        gain_first.reshape(1, 128),
        conv_weight.reshape(27, 128, 128),
        gain_second.reshape(1, 128),
        out_weight.T,
        disc_first[0].transpose(0, 2, 1, 3).reshape(12, 4, 64),
        disc_second.reshape(32, 64, 128),
        score_grad[0],
        *picks,
    )
    input_grad, update = pl.pallas_call(
        finish_kernel,
        out_shape=(
            jax.ShapeDtypeStruct((4, 8, 32, 128), LOW),
            jax.ShapeDtypeStruct((2, 1728, 128), WIDE),
        ),
        in_specs=[vmem] * 3,
        out_specs=(vmem, vmem),
        compiler_params=pltpu.CompilerParams(vmem_limit_bytes=64 * 1024 * 1024),
    )(input_grad, summed, scale)
    return (input_grad[None], update.reshape(conv_weight.shape))


def solution(mesh):
    split = P("batch", "frame", "row", None, None)
    in_specs = (split, P(), P(), P(), P(), P(), P(), split)
    return jax.shard_map(
        shards, mesh=mesh, in_specs=in_specs, out_specs=(split, P()), check_vma=False
    )
```

```python
import jax
import jax.numpy as jnp
import numpy as np
from jax import lax
from jax.experimental import pallas as pl
from jax.experimental.pallas import tpu as pltpu
from jax.sharding import PartitionSpec as P

EPSILON = 1e-06
LOW = jnp.bfloat16
WIDE = jnp.float32
LOCAL = 1024
PER_CLIP = 64


def group_total(values):
    lane = lax.broadcasted_iota(jnp.int32, values.shape, 1)
    paired = values + jnp.where(
        lane % 2 == 0, pltpu.roll(values, 127, 1), pltpu.roll(values, 1, 1)
    )
    return paired + jnp.where(
        lane % 4 < 2, pltpu.roll(paired, 126, 1), pltpu.roll(paired, 2, 1)
    )


def tile(row):
    return jnp.broadcast_to(row, (8, row.shape[-1]))


def silu_slope(values):
    logistic = jax.nn.sigmoid(values)
    return logistic * (1.0 + values * (1.0 - logistic))


def place():
    batch = lax.axis_index("batch")
    row = lax.axis_index("row")
    return dict(
        batch=batch,
        z_lo=batch // 2,
        core=batch % 2,
        frame=lax.axis_index("frame"),
        row=row,
        z_hi=row // 4,
        y=row % 4,
    )


def device(me, **changed):
    at = dict(me, **changed)
    return (at["z_lo"] * 2 + at["core"], at["frame"], at["z_hi"] * 4 + at["y"])


def neighbour(me, frame_step, row_step):
    return (me["batch"], (me["frame"] + frame_step) % 4, (me["row"] + row_step) % 16)


def plane_peers(me):
    own = me["frame"] * 4 + me["y"]
    others = [(own + step) % 16 for step in range(1, 16)]
    return [(other, device(me, frame=other // 4, y=other % 4)) for other in others]


def z_peers(me):
    own = me["z_hi"] * 4 + me["z_lo"]
    others = [(own + step) % 16 for step in range(1, 16)]
    return [(other, device(me, z_hi=other // 4, z_lo=other % 4)) for other in others]


def clip_peers(me):
    return [
        device(
            me,
            z_hi=(me["z_hi"] + dz) % 4,
            y=(me["y"] + dy) % 4,
            frame=(me["frame"] + dx) % 4,
        )
        for dz in (2, 1, 3, 0)
        for dy in (2, 1, 3, 0)
        for dx in (2, 1, 3, 0)
        if (dz, dy, dx) != (0, 0, 0)
    ]


def high_peers(me):
    others = [(me["z_hi"] + step) % 4 for step in range(1, 4)]
    return [(other, device(me, z_hi=other)) for other in others]


def push(src, dst, peer, send_sem, recv_sem):
    pltpu.make_async_remote_copy(
        src_ref=src,
        dst_ref=dst,
        send_sem=send_sem,
        recv_sem=recv_sem,
        device_id=peer,
        device_id_type=pl.DeviceIdType.MESH,
    ).start()


def arrived(like, sem):
    pltpu.make_async_copy(like, like, sem).wait()


def selections():
    rows_first = np.zeros((160, 96), np.float32)
    for k in range(4):
        for a in range(10):
            for t in range(4):
                block, r = divmod(2 * a + k + 1, 8)
                rows_first[k * 40 + a * 4 + t, block * 32 + t * 8 + r] = 1
    rows_second = np.zeros((64, 40), np.float32)
    for m in range(2):
        for k in range(4):
            for u in range(2):
                for b in range(4):
                    rows_second[(m * 4 + k) * 8 + u * 4 + b, (2 * b + k) * 4 + 2 * u + m] = 1
    rows_back = np.zeros((32, 96), np.float32)
    for k in range(4):
        for a in range(2, 8):
            for t in range(4):
                r = 2 * a + k - 7
                if 0 <= r < 8:
                    rows_back[t * 8 + r, k * 24 + (a - 2) * 4 + t] = 1
    return (
        jnp.asarray(rows_first, LOW),
        jnp.asarray(rows_second, LOW),
        jnp.asarray(rows_second.T[8:32].copy(), WIDE),
        jnp.asarray(rows_back, WIDE),
    )


def column_sum(left, middle, right):
    column = lax.broadcasted_iota(jnp.int32, middle.shape, 0) % 32
    rows = middle.shape[0]
    return (
        middle
        + jnp.where(column == 0, 0.0, pltpu.roll(left, 1, 0))
        + jnp.where(column == 31, 0.0, pltpu.roll(right, rows - 1, 0))
    )


def across(left, right):
    return lax.dot_general(left, right, (((1,), (1,)), ((), ())), preferred_element_type=WIDE)


def wide_dot(left, right):
    return jnp.dot(left, right, preferred_element_type=WIDE)


def exact_pick(pick, values):
    return jnp.dot(pick, values, precision=lax.Precision.HIGHEST, preferred_element_type=WIDE)


def step_kernel(
    x_hbm, gain1_hbm, w_hbm, gain2_hbm, ow_hbm, d1_hbm, d2_hbm, score_hbm,
    pick_first_hbm, pick_second_hbm, pick_second_back_hbm, pick_first_back_hbm,
    grad_hbm, summed_hbm, scale_ref,
    out_ref, gain1_ref, w_ref, gain2_ref, ow_ref, d1_ref, d2_ref,
    pick_first, pick_second, pick_second_back, pick_first_back,
    xe, ae, ge, mx, ag, wg, xt, g3, w_fwd, w_back,
    ow_f, ow_cols, ow_rows, d1_f, d1_rows, images, sg, sg_flat,
    dw, p1, reach, pair_out, pair_in, plane_out, plane_in, z_out, z_in, z_all, gathered,
    stats, plane, high, load_sem,
    stat_send, stat_recv, halo_send, halo_recv, sum_send, sum_recv,
):
    me = place()
    frame, row, core, y, z_hi = (me["frame"], me["row"], me["core"], me["y"], me["z_hi"])
    z = z_hi * 4 + me["z_lo"]
    slot = frame * 4 + y
    clip_slot = row * 4 + frame
    clip_line = clip_peers(me)
    plane_line, z_line, high_line = (plane_peers(me), z_peers(me), high_peers(me))
    partner = device(me, core=1 - core)
    above, below = (neighbour(me, 0, -1), neighbour(me, 0, 1))

    barrier = pltpu.get_barrier_semaphore()
    greeted = clip_line + [partner] + [
        device(me, z_hi=(z_hi + dz) % 4, z_lo=(me["z_lo"] + dl) % 4)
        for dz in range(4)
        for dl in range(1, 4)
    ]
    for peer in greeted:
        pl.semaphore_signal(
            barrier, inc=1, device_id=peer, device_id_type=pl.DeviceIdType.MESH
        )

    own_strip = (pl.ds(2, 4), pl.ds(1, 8))
    loads = [
        (x_hbm, xe.at[own_strip]),
        (score_hbm, sg.at[:, pl.ds(1, 2)]),
        (w_hbm, w_ref),
        (ow_hbm, ow_ref),
        (d1_hbm, d1_ref),
        (gain1_hbm, gain1_ref),
        (gain2_hbm, gain2_ref),
        (d2_hbm, d2_ref),
        (pick_first_hbm, pick_first),
        (pick_second_hbm, pick_second),
        (pick_second_back_hbm, pick_second_back),
        (pick_first_back_hbm, pick_first_back),
    ]
    loads = [
        pltpu.make_async_copy(src, dst, load_sem.at[index])
        for index, (src, dst) in enumerate(loads)
    ]
    for load in loads:
        load.start()

    def stats_start(turn, first, second, before_nearest=lambda: None):
        stats[turn, clip_slot, 0:1, :] = first
        stats[turn, clip_slot, 1:2, :] = second
        mine = stats.at[turn, clip_slot]
        for index, peer in enumerate(clip_line):
            if index == 48:
                before_nearest()
            push(mine, mine, peer, stat_send.at[turn], stat_recv.at[turn])

    def stats_wait(turn):
        others = stats.at[turn, pl.ds(0, 63)]
        arrived(others, stat_recv.at[turn])
        arrived(others, stat_send.at[turn])

    def moments_end(turn):
        stats_wait(turn)
        parts = stats[turn]
        sums = jnp.sum(parts, axis=0)
        mean = group_total(tile(sums[0:1])) / (4.0 * PER_CLIP)
        apart = parts - mean[0:2]
        spread = jnp.sum(apart * apart, axis=0)
        total = group_total(tile(sums[1:2] + float(LOCAL) * spread[0:1]))
        return (mean[0:1], lax.rsqrt(total[0:1] / (4.0 * LOCAL * PER_CLIP) + EPSILON))

    def sums_end(turn):
        stats_wait(turn)
        sums = jnp.sum(stats[turn], axis=0) / (4.0 * LOCAL * PER_CLIP)
        return (group_total(tile(sums[0:1]))[0:1], group_total(tile(sums[1:2]))[0:1])

    def plane_start(first, second):
        plane[slot, 0:1, :] = first
        plane[slot, 1:2, :] = second
        for _, peer in plane_line:
            push(plane.at[slot], plane.at[slot], peer, stat_send.at[3], stat_recv.at[3])

    def plane_to_high():
        others = plane.at[pl.ds(0, 15)]
        arrived(others, stat_recv.at[3])
        arrived(others, stat_send.at[3])
        high[z_hi] = jnp.sum(plane[...], axis=0)
        for _, peer in high_line:
            push(high.at[z_hi], high.at[z_hi], peer, stat_send.at[4], stat_recv.at[4])

    def high_end():
        others = high.at[pl.ds(0, 3)]
        arrived(others, stat_recv.at[4])
        arrived(others, stat_send.at[4])
        sums = jnp.sum(high[...], axis=0) / (4.0 * LOCAL * PER_CLIP)
        return (group_total(tile(sums[0:1]))[0:1], group_total(tile(sums[1:2]))[0:1])

    def local_moments(read):
        zero = jnp.zeros((1, 128), WIDE)
        total = lax.fori_loop(
            0, 4, lambda t, acc: acc + jnp.sum(read(t), axis=0, keepdims=True), zero
        )
        mean = total / float(LOCAL)

        def squares(t, acc):
            apart = read(t) - mean
            return acc + jnp.sum(apart * apart, axis=0, keepdims=True)

        return (mean, lax.fori_loop(0, 4, squares, zero))

    def column_copies(t, values):
        here = pl.ds(t * 256, 256)
        values = values.astype(LOW)
        wide = values.astype(WIDE)
        column = lax.broadcasted_iota(jnp.int32, wide.shape, 0) % 32
        g3[here, 128:256] = values
        g3[here, 0:128] = jnp.where(column == 31, 0.0, pltpu.roll(wide, 255, 0)).astype(LOW)
        g3[here, 256:384] = jnp.where(column == 0, 0.0, pltpu.roll(wide, 1, 0)).astype(LOW)

    def acts_window(i, j):
        return jnp.concatenate([xt[j, i + t] for t in range(4)], axis=1)

    def against_acts(result):
        for i in range(3):
            for j in range(3):
                product = wide_dot(acts_window(i, j), g3[...])
                for c in range(3):
                    first = ((i * 3 + j) * 3 + c) * 128
                    result[first : first + 128, :] = product[:, c * 128 : (c + 1) * 128]

    def halo_start(turn, src, dst, own_row, own_frames, to_frames, frame_step):
        def go(index, source, target, peer):
            push(source, target, peer, halo_send.at[turn, index], halo_recv.at[turn, index])

        inner = pl.ds(own_frames[0], 4)
        edge = pl.ds(own_frames[1], 2)
        base = pl.ds(own_frames[2], 4)
        far = pl.ds(to_frames, 2)
        go(0, src.at[inner, own_row + 7], dst.at[base, 0], below)
        go(1, src.at[inner, own_row], dst.at[base, 9], above)
        go(2, src.at[edge, pl.ds(own_row, 8)], dst.at[far, pl.ds(1, 8)], neighbour(me, frame_step, 0))
        go(3, src.at[edge, own_row + 7], dst.at[far, 0], neighbour(me, frame_step, 1))
        go(4, src.at[edge, own_row], dst.at[far, 9], neighbour(me, frame_step, -1))

    def halo_wait(turn, dst, base_frame, to_frames):
        base = pl.ds(base_frame, 4)
        far = pl.ds(to_frames, 2)
        parts = [
            dst.at[base, 0],
            dst.at[base, 9],
            dst.at[far, pl.ds(1, 8)],
            dst.at[far, 0],
            dst.at[far, 9],
        ]
        for index, part in enumerate(parts):
            arrived(part, halo_recv.at[turn, index])
            arrived(part, halo_send.at[turn, index])

    def inside(shape, outside_frame):
        position = lax.broadcasted_iota(jnp.int32, shape, 0)
        low = jnp.where(row == 0, 32, 0)
        high_end = jnp.where(row == 15, 288, 320)
        high_end = jnp.where(outside_frame, 0, high_end)
        return (position >= low) & (position < high_end)

    def own_input(t):
        return xe[t + 2, 1:9].astype(WIDE).reshape(256, 128)

    loads[0].wait()
    mean, squares = local_moments(own_input)
    loads[1].wait()
    pl.semaphore_wait(barrier, len(greeted))
    stats_start(0, mean, squares, lambda: halo_start(0, xe, xe, 1, (2, 4, 2), 0, 1))
    push(sg.at[:, 2], sg.at[:, 0], below, halo_send.at[0, 5], halo_recv.at[0, 5])
    push(sg.at[:, 1], sg.at[:, 3], above, halo_send.at[0, 6], halo_recv.at[0, 6])
    for load in loads[2:]:
        load.wait()

    @pl.loop(0, 9)
    def _(tap):
        for c in range(3):
            w_fwd[pl.ds(tap * 128, 128), c * 128 : (c + 1) * 128] = w_ref[tap * 3 + c]

    ow_f[...] = jnp.zeros((128, 128), WIDE)
    ow_f[0:3, :] = ow_ref[...].astype(WIDE)
    colours_t = ow_f[...]
    colours = colours_t.T
    for c in range(32):
        ow_cols[c * 128 : (c + 1) * 128, :] = (
            colours if c == 0 else pltpu.roll(colours, 3 * c, 1)
        ).astype(LOW)
        ow_rows[:, c * 128 : (c + 1) * 128] = (
            colours_t if c == 0 else pltpu.roll(colours_t, 3 * c, 0)
        ).astype(LOW)
    for k in range(4):
        d1_f[...] = jnp.zeros((128, 128), WIDE)
        for colour in range(3):
            taps = d1_ref[k * 3 + colour].astype(WIDE)
            for l in range(4):
                d1_f[3 * l + colour : 3 * l + colour + 1, 0:64] = taps[l : l + 1]
        single = d1_f[...]
        double = single + pltpu.roll(pltpu.roll(single, 64, 1), 6, 0)
        for p in range(8):
            d1_rows[k * 128 : (k + 1) * 128, p * 128 : (p + 1) * 128] = pltpu.roll(
                double, (12 * p - 3) % 128, 0
            ).astype(LOW)

    @pl.loop(0, 9)
    def _(tap):
        for c in range(3):
            w_back[pl.ds(tap * 128, 128), c * 128 : (c + 1) * 128] = (
                w_ref[tap * 3 + c].astype(WIDE).T.astype(LOW)
            )

    halo_wait(0, xe, 2, 0)
    for index in (5, 6):
        arrived(sg.at[:, 0], halo_recv.at[0, index])
        arrived(sg.at[:, 0], halo_send.at[0, index])
    gain1 = gain1_ref[...]
    gain2 = gain2_ref[...]
    mean1, inverse1 = moments_end(0)

    @pl.loop(0, 6)
    def _(t):
        scaled = (xe[t].astype(WIDE).reshape(320, 128) - mean1) * inverse1 * gain1
        act = scaled * jax.nn.sigmoid(scaled)
        keep = inside(act.shape, (t < 2) & (frame == 0))
        ae[t] = jnp.where(keep, act, 0.0).astype(LOW).reshape(10, 32, 128)

    @pl.loop(0, 4)
    def _(t):
        taps = [ae[t + i, j : j + 8].reshape(256, 128) for i in range(3) for j in range(3)]
        product = wide_dot(jnp.concatenate(taps, axis=1), w_fwd[...])
        branch = column_sum(product[:, 0:128], product[:, 128:256], product[:, 256:384])
        mx[t] = (xe[t + 2, 1:9].astype(WIDE).reshape(256, 128) + branch).astype(LOW)

    mean, squares = local_moments(lambda t: mx[t].astype(WIDE))
    stats_start(1, mean, squares)

    @pl.loop(0, 6)
    def _(t):
        for j in range(3):
            xt[j, t] = ae[t, j : j + 8].reshape(256, 128).astype(WIDE).T.astype(LOW)

    column = lax.broadcasted_iota(jnp.int32, (1024, 128), 0) % 32
    tap_lane = lax.broadcasted_iota(jnp.int32, (1024, 128), 1)
    reached = ((tap_lane != 0) | (column < 31)) & ((tap_lane != 2) | (column > 0))
    reached = jnp.where(reached, 1.0, 0.0).astype(LOW)
    for i in range(3):
        for j in range(3):
            reach[i * 3 + j] = wide_dot(acts_window(i, j), reached)

    mean2, inverse2 = moments_end(1)

    def normed_second(t):
        return (mx[t].astype(WIDE) - mean2) * inverse2

    @pl.loop(0, 4)
    def _(t):
        scaled = normed_second(t) * gain2
        act = (scaled * jax.nn.sigmoid(scaled)).astype(LOW)
        ag[pl.ds(t * 256, 256), :] = act.astype(WIDE)

    image = jnp.zeros((32, 128), WIDE)
    for part in range(4):
        columns = [ag[pl.ds(c, 32, stride=32), :] for c in range(part * 8, part * 8 + 8)]
        image = image + wide_dot(
            jnp.concatenate(columns, axis=1).astype(LOW), ow_cols[part * 1024 : (part + 1) * 1024, :]
        )
    images[1] = image.astype(LOW)
    push(images.at[1], images.at[0], below, halo_send.at[1, 5], halo_recv.at[1, 5])
    push(images.at[1], images.at[2], above, halo_send.at[1, 6], halo_recv.at[1, 6])

    @pl.loop(0, 4)
    def _(t):
        column_copies(t, normed_second(t))

    against_acts(p1)
    sg_flat[...] = sg[...].reshape(64, 128)
    score = jnp.concatenate([sg_flat[pl.ds(p, 8, stride=8), :] for p in range(8)], axis=0)
    for index in (5, 6):
        arrived(images.at[0], halo_recv.at[1, index])
        arrived(images.at[0], halo_send.at[1, index])

    strips = jnp.concatenate(
        [
            jnp.where(row == 0, 0.0, images[0].astype(WIDE)),
            images[1].astype(WIDE),
            jnp.where(row == 15, 0.0, images[2].astype(WIDE)),
        ],
        axis=0,
    ).astype(LOW)
    picked = wide_dot(pick_first[...], strips)
    taps = [picked[k * 40 : (k + 1) * 40] for k in range(4)]
    first_pre = wide_dot(jnp.concatenate(taps, axis=1).astype(LOW), d1_rows[...])
    place_row = lax.broadcasted_iota(jnp.int32, first_pre.shape, 0)
    low_row = jnp.where(row == 0, 12, 0)
    high_row = jnp.where(row == 15, 28, 40)
    real = (place_row >= low_row) & (place_row < high_row)
    first_act = jnp.where(real, first_pre * jax.nn.sigmoid(first_pre), 0.0).astype(LOW)
    picked = wide_dot(pick_second[...], first_act)
    blank = jnp.zeros((8, 128), WIDE)
    lane = lax.broadcasted_iota(jnp.int32, (64, 128), 1)
    second_pre = jnp.zeros((64, 128), WIDE)
    for tap in range(8):
        middle = jnp.concatenate(
            [picked[tap * 8 : tap * 8 + 8, p * 128 : (p + 1) * 128] for p in range(8)], axis=0
        )
        turned = pltpu.roll(middle, 64, 1)
        sides = jnp.where(
            lane < 64,
            jnp.concatenate([blank, turned[0:56]], axis=0),
            jnp.concatenate([turned[8:64], blank], axis=0),
        )
        weights = jnp.concatenate([d2_ref[tap * 4 + l] for l in (1, 2, 0, 3)], axis=0)
        second_pre = second_pre + wide_dot(
            jnp.concatenate([middle, sides], axis=1).astype(LOW), weights
        )
    strip = lax.broadcasted_iota(jnp.int32, (64, 128), 0) % 4
    first_strip = jnp.where(row == 0, 1, 0)
    last_strip = jnp.where(row == 15, 2, 3)
    score_pre = jnp.where(
        (strip >= first_strip) & (strip <= last_strip), score * silu_slope(second_pre), 0.0
    ).astype(LOW).astype(WIDE)
    sources = jnp.concatenate(
        [
            score_pre,
            jnp.concatenate([blank, score_pre[0:56]], axis=0),
            jnp.concatenate([score_pre[8:64], blank], axis=0),
        ],
        axis=1,
    ).astype(LOW)
    nothing = jnp.zeros((64, 128), LOW)
    spread = []
    for tap in range(8):
        even = jnp.concatenate([d2_ref[tap * 4 + 1], d2_ref[tap * 4 + 3], nothing], axis=1)
        odd = jnp.concatenate([d2_ref[tap * 4 + 2], nothing, d2_ref[tap * 4]], axis=1)
        back = across(sources, jnp.concatenate([even, odd], axis=0))
        spread.append(
            jnp.concatenate([back[p * 8 : (p + 1) * 8] for p in range(8)], axis=1)
        )
    first_full = exact_pick(pick_second_back[...], jnp.concatenate(spread, axis=0))
    first_grad = jnp.where(real[8:32], first_full * silu_slope(first_pre[8:32]), 0.0).astype(LOW)
    back = across(first_grad, d1_rows[...])
    stacked = jnp.concatenate([back[:, k * 128 : (k + 1) * 128] for k in range(4)], axis=0)
    image_grad = exact_pick(pick_first_back[...], stacked).astype(LOW)
    for part in range(4):
        grads = wide_dot(image_grad, ow_rows[:, part * 1024 : (part + 1) * 1024])
        for c in range(8):
            ag[pl.ds(part * 8 + c, 32, stride=32), :] = grads[:, c * 128 : (c + 1) * 128]

    def weigh(t, acc):
        normed = normed_second(t)
        here = pl.ds(t * 256, 256)
        weighted = ag[here, :] * silu_slope(normed * gain2) * gain2
        ag[here, :] = weighted
        column_copies(t, weighted * inverse2)
        return (
            acc[0] + jnp.sum(weighted, axis=0, keepdims=True),
            acc[1] + jnp.sum(weighted * normed, axis=0, keepdims=True),
        )

    zeros = (jnp.zeros((1, 128), WIDE), jnp.zeros((1, 128), WIDE))
    sums = lax.fori_loop(0, 4, weigh, zeros)
    stats_start(2, *sums)
    against_acts(dw)
    first_mean, second_mean = sums_end(2)

    @pl.loop(0, 4)
    def _(t):
        here = pl.ds(t * 256, 256)
        grad = (ag[here, :] - first_mean - normed_second(t) * second_mean) * inverse2
        ag[here, :] = grad
        ge[t, 1:9] = grad.astype(LOW).reshape(8, 32, 128)

    halo_start(1, ge, ge, 1, (0, 0, 0), 4, -1)

    first_part, second_part = (first_mean * inverse2, second_mean * inverse2)
    for i in range(9):
        for c in range(3):
            rows = slice((i * 3 + c) * 128, (i * 3 + c) * 128 + 128)
            dw[rows, :] = (
                dw[rows, :] - reach[i, :, c : c + 1] * first_part - p1[rows, :] * second_part
            )
    dw[3456:3520, :] = jnp.zeros((64, 128), WIDE)
    theirs = pl.ds(pl.multiple_of((1 - core) * 1728, 64), 1792)
    ours = pl.ds(pl.multiple_of(core * 1728, 64), 1792)
    chunks = (pl.ds(0, 64), pl.ds(64, 48))
    pair_out[...] = dw[theirs, :].astype(LOW).reshape(16, 112, 128)
    for turn, chunk in enumerate(chunks):
        push(pair_out.at[:, chunk], pair_in.at[:, chunk], partner, sum_send.at[turn], sum_recv.at[turn])

    for turn, chunk in enumerate(chunks):
        arrived(pair_in.at[:, chunk], sum_recv.at[turn])
        arrived(pair_in.at[:, chunk], sum_send.at[turn])
        mine = dw[ours, :].reshape(16, 112, 128)[:, chunk.start : chunk.start + chunk.size]
        plane_out[:, chunk] = (mine + pair_in[:, chunk].astype(WIDE)).astype(LOW)
        for other, peer in plane_line:
            push(
                plane_out.at[other, chunk],
                plane_in.at[slot, chunk],
                peer,
                sum_send.at[2 + turn],
                sum_recv.at[2 + turn],
            )
        plane_in[slot, chunk] = plane_out[slot, chunk]

    tiles = (range(0, 4), range(4, 7))
    own_tile = z % 8
    owns = (own_tile < 4, (own_tile >= 4) & (own_tile < 7))
    for turn, chunk in enumerate(chunks):
        others = plane_in.at[pl.ds(0, 15), chunk]
        arrived(others, sum_recv.at[2 + turn])
        arrived(others, sum_send.at[2 + turn])
        total = jnp.sum(plane_in[:, chunk].astype(WIDE), axis=0).astype(LOW)
        for index, part in enumerate(tiles[turn]):
            z_out[part] = total[index * 16 : (index + 1) * 16]
            for owner in (part, part + 8):

                @pl.when(z != owner)
                def _():
                    push(
                        z_out.at[part],
                        z_in.at[z],
                        device(me, z_hi=owner // 4, z_lo=owner % 4),
                        sum_send.at[4 + turn],
                        sum_recv.at[4],
                    )

    halo_wait(1, ge, 0, 4)

    def normed_first(t):
        return (own_input(t) - mean1) * inverse1

    def back_step(t, acc):
        taps = []
        for i in range(3):
            for j in range(3):
                strip = ge[t + 2 - i, 2 - j : 10 - j].reshape(256, 128)
                above_edge = (row == 0) if j == 2 else False
                below_edge = (row == 15) if j == 0 else False
                late = (frame == 3) & (t + 2 - i > 3)
                position = lax.broadcasted_iota(jnp.int32, (256, 128), 0)
                low = jnp.where(above_edge, 32, 0)
                end = jnp.where(late, 0, jnp.where(below_edge, 224, 256))
                keep = (position >= low) & (position < end)
                taps.append(jnp.where(keep, strip.astype(WIDE), 0.0).astype(LOW))
        product = wide_dot(jnp.concatenate(taps, axis=1), w_back[...])
        grad = column_sum(product[:, 256:384], product[:, 128:256], product[:, 0:128])
        normed = normed_first(t)
        weighted = grad * silu_slope(normed * gain1) * gain1
        wg[t] = weighted
        return (
            acc[0] + jnp.sum(weighted, axis=0, keepdims=True),
            acc[1] + jnp.sum(weighted * normed, axis=0, keepdims=True),
        )

    sums = lax.fori_loop(0, 4, back_step, zeros)
    plane_start(*sums)

    for turn in range(2):

        @pl.when(owns[turn])
        def _():
            z_in[z] = z_out[own_tile]
            arrived(z_in.at[pl.ds(0, 15)], sum_recv.at[4])
            z_all[own_tile] = jnp.sum(z_in[...].astype(WIDE), axis=0).astype(LOW)
            mine = z_all.at[own_tile]
            for step in (-4, 3, -3, 2, -2, 1, -1):
                other = (z + step) % 16
                peer = device(me, z_hi=other // 4, z_lo=other % 4)
                push(mine, mine, peer, sum_send.at[6], sum_recv.at[6 + turn])

    plane_to_high()

    half, other_half = (gathered.at[core], gathered.at[1 - core])
    for turn, chunk in enumerate(chunks):
        count = len(tiles[turn])

        @pl.when(owns[turn])
        def _():
            arrived(z_all.at[pl.ds(0, count - 1)], sum_recv.at[6 + turn])
            arrived(z_in.at[pl.ds(0, 2 * count - 1)], sum_send.at[4 + turn])
            arrived(z_in.at[pl.ds(0, 7)], sum_send.at[6])

        @pl.when(jnp.logical_not(owns[turn]))
        def _():
            arrived(z_all.at[pl.ds(0, count)], sum_recv.at[6 + turn])
            arrived(z_in.at[pl.ds(0, 2 * count)], sum_send.at[4 + turn])

        first = tiles[turn].start
        half[slot, chunk] = z_all[first : first + count].reshape(count * 16, 128)
        for _, peer in plane_line:
            push(
                half.at[slot, chunk],
                half.at[slot, chunk],
                peer,
                sum_send.at[8 + turn],
                sum_recv.at[8 + turn],
            )

    first_mean, second_mean = high_end()

    @pl.loop(0, 4)
    def _(t):
        grad = (wg[t] - first_mean - normed_first(t) * second_mean) * inverse1
        out_ref[t] = (ag[pl.ds(t * 256, 256), :] + grad).astype(LOW).reshape(8, 32, 128)

    out_copy = pltpu.make_async_copy(out_ref, grad_hbm, load_sem.at[12])
    out_copy.start()

    def squares_of(part_of, chunk):
        def add(part, acc):
            piece = part_of[part, chunk].astype(WIDE)
            return acc + jnp.sum((piece * piece).reshape(chunk.size // 8, 8, 128), axis=0)

        total = lax.fori_loop(0, 15, add, jnp.zeros((8, 128), WIDE))
        if chunk.start == 0:
            piece = part_of[15, 0:48].astype(WIDE)
            total = total + jnp.sum((piece * piece).reshape(6, 8, 128), axis=0)
        return total

    squares = []
    for turn, chunk in enumerate(chunks):
        others = half.at[pl.ds(0, 15), chunk]
        arrived(others, sum_recv.at[8 + turn])
        arrived(others, sum_send.at[8 + turn])
        push(half.at[:, chunk], half.at[:, chunk], partner, sum_send.at[10 + turn], sum_recv.at[10 + turn])
        squares.append(squares_of(half, chunk))
    own_copy = pltpu.make_async_copy(half, summed_hbm.at[core], load_sem.at[13])
    own_copy.start()
    for turn, chunk in enumerate(chunks):
        arrived(other_half.at[:, chunk], sum_recv.at[10 + turn])
        arrived(half.at[:, chunk], sum_send.at[10 + turn])
    other_copy = pltpu.make_async_copy(other_half, summed_hbm.at[1 - core], load_sem.at[14])
    other_copy.start()
    for chunk in chunks:
        squares.append(squares_of(other_half, chunk))
    total = (squares[0] + squares[1]) + (squares[2] + squares[3])
    mean = jnp.sum(total, keepdims=True) / (3456.0 * 128.0)
    scale_ref[...] = jnp.broadcast_to(lax.rsqrt(mean + EPSILON), (8, 128))
    for copy in (out_copy, own_copy, other_copy):
        copy.wait()


def finish_kernel(grad_ref, summed_ref, scale_ref, out_ref, upd_ref):
    out_ref[...] = grad_ref[...]
    scale = scale_ref[0:1, :]
    values = summed_ref[0, 0:15].reshape(1680, 128)
    upd_ref[0, 0:1680, :] = values.astype(WIDE) * scale
    upd_ref[0, 1680:1728, :] = summed_ref[0, 15, 0:48].astype(WIDE) * scale


def shards(
    block_input, gain_first, conv_weight, gain_second, out_weight, disc_first, disc_second, score_grad
):
    vmem = pl.BlockSpec(memory_space=pltpu.VMEM)
    low = lambda *shape: pltpu.VMEM(shape, LOW)
    wide = lambda *shape: pltpu.VMEM(shape, WIDE)
    dma = pltpu.SemaphoreType.DMA
    picks = selections()
    hbm = pl.BlockSpec(memory_space=pltpu.HBM)
    input_grad, summed, scale = pl.pallas_call(
        step_kernel,
        out_shape=(
            jax.ShapeDtypeStruct((4, 8, 32, 128), LOW),
            jax.ShapeDtypeStruct((2, 16, 112, 128), LOW),
            jax.ShapeDtypeStruct((8, 128), WIDE),
        ),
        in_specs=[hbm] * 12,
        out_specs=(hbm, hbm, vmem),
        scratch_shapes=[
            low(4, 8, 32, 128), wide(1, 128), low(27, 128, 128), wide(1, 128), low(3, 128), low(12, 4, 64),
            low(32, 64, 128), low(160, 96), low(64, 40), wide(24, 64), wide(32, 96),
            low(6, 10, 32, 128), low(6, 10, 32, 128), low(6, 10, 32, 128),
            low(4, 256, 128), wide(1024, 128), wide(4, 256, 128),
            low(3, 6, 128, 256), low(1024, 384), low(1152, 384), low(1152, 384),
            wide(128, 128), low(4096, 128), low(128, 4096), wide(128, 128), low(512, 1024),
            low(3, 32, 128), wide(2, 4, 8, 128), wide(64, 128),
            wide(3520, 128), wide(3456, 128), wide(9, 128, 128), low(16, 112, 128), low(16, 112, 128), low(16, 112, 128), low(16, 112, 128),
            low(7, 16, 128), low(16, 16, 128), low(7, 16, 128), low(2, 16, 112, 128),
            wide(3, 64, 2, 128), wide(16, 2, 128), wide(4, 2, 128),
            dma((15,)), dma((5,)), dma((5,)), dma((2, 7)), dma((2, 7)), dma((12,)), dma((12,)),
        ],
        compiler_params=pltpu.CompilerParams(
            collective_id=1, has_side_effects=True, vmem_limit_bytes=64 * 1024 * 1024
        ),
    )(
        block_input[0],
        gain_first.reshape(1, 128),
        conv_weight.reshape(27, 128, 128),
        gain_second.reshape(1, 128),
        out_weight.T,
        disc_first[0].transpose(0, 2, 1, 3).reshape(12, 4, 64),
        disc_second.reshape(32, 64, 128),
        score_grad[0],
        *picks,
    )
    input_grad, update = pl.pallas_call(
        finish_kernel,
        out_shape=(
            jax.ShapeDtypeStruct((4, 8, 32, 128), LOW),
            jax.ShapeDtypeStruct((2, 1728, 128), WIDE),
        ),
        grid=(2,),
        in_specs=[
            pl.BlockSpec((2, 8, 32, 128), lambda half: (half, 0, 0, 0)),
            pl.BlockSpec((1, 16, 112, 128), lambda half: (half, 0, 0, 0)),
            pl.BlockSpec((8, 128), lambda half: (0, 0)),
        ],
        out_specs=(
            pl.BlockSpec((2, 8, 32, 128), lambda half: (half, 0, 0, 0)),
            pl.BlockSpec((1, 1728, 128), lambda half: (half, 0, 0)),
        ),
        compiler_params=pltpu.CompilerParams(vmem_limit_bytes=64 * 1024 * 1024),
    )(input_grad, summed, scale)
    return (input_grad[None], update.reshape(conv_weight.shape))


def solution(mesh):
    split = P("batch", "frame", "row", None, None)
    in_specs = (split, P(), P(), P(), P(), P(), P(), split)
    return jax.shard_map(
        shards, mesh=mesh, in_specs=in_specs, out_specs=(split, P()), check_vma=False
    )
```

```python
import jax
import jax.numpy as jnp
import numpy as np
from jax import lax
from jax.experimental import pallas as pl
from jax.experimental.pallas import tpu as pltpu
from jax.sharding import PartitionSpec as P

EPSILON = 1e-06
LOW = jnp.bfloat16
WIDE = jnp.float32
LOCAL = 1024
PER_CLIP = 64


def group_total(values):
    lane = lax.broadcasted_iota(jnp.int32, values.shape, 1)
    paired = values + jnp.where(
        lane % 2 == 0, pltpu.roll(values, 127, 1), pltpu.roll(values, 1, 1)
    )
    return paired + jnp.where(
        lane % 4 < 2, pltpu.roll(paired, 126, 1), pltpu.roll(paired, 2, 1)
    )


def tile(row):
    return jnp.broadcast_to(row, (8, row.shape[-1]))


def silu_slope(values):
    logistic = jax.nn.sigmoid(values)
    return logistic * (1.0 + values * (1.0 - logistic))


def place():
    batch = lax.axis_index("batch")
    row = lax.axis_index("row")
    return dict(
        batch=batch,
        z_lo=batch // 2,
        core=batch % 2,
        frame=lax.axis_index("frame"),
        row=row,
        z_hi=row // 4,
        y=row % 4,
    )


def device(me, **changed):
    at = dict(me, **changed)
    return (at["z_lo"] * 2 + at["core"], at["frame"], at["z_hi"] * 4 + at["y"])


def neighbour(me, frame_step, row_step):
    return (me["batch"], (me["frame"] + frame_step) % 4, (me["row"] + row_step) % 16)


def plane_peers(me):
    own = me["frame"] * 4 + me["y"]
    others = [(own + step) % 16 for step in range(1, 16)]
    return [(other, device(me, frame=other // 4, y=other % 4)) for other in others]


def z_peers(me):
    own = me["z_hi"] * 4 + me["z_lo"]
    others = [(own + step) % 16 for step in range(1, 16)]
    return [(other, device(me, z_hi=other // 4, z_lo=other % 4)) for other in others]


def clip_peers(me):
    return [
        device(
            me,
            z_hi=(me["z_hi"] + dz) % 4,
            y=(me["y"] + dy) % 4,
            frame=(me["frame"] + dx) % 4,
        )
        for dz in (2, 1, 3, 0)
        for dy in (2, 1, 3, 0)
        for dx in (2, 1, 3, 0)
        if (dz, dy, dx) != (0, 0, 0)
    ]


def high_peers(me):
    others = [(me["z_hi"] + step) % 4 for step in range(1, 4)]
    return [(other, device(me, z_hi=other)) for other in others]


def push(src, dst, peer, send_sem, recv_sem):
    pltpu.make_async_remote_copy(
        src_ref=src,
        dst_ref=dst,
        send_sem=send_sem,
        recv_sem=recv_sem,
        device_id=peer,
        device_id_type=pl.DeviceIdType.MESH,
    ).start()


def arrived(like, sem):
    pltpu.make_async_copy(like, like, sem).wait()


def selections():
    rows_first = np.zeros((160, 96), np.float32)
    for k in range(4):
        for a in range(10):
            for t in range(4):
                block, r = divmod(2 * a + k + 1, 8)
                rows_first[k * 40 + a * 4 + t, block * 32 + t * 8 + r] = 1
    rows_second = np.zeros((64, 40), np.float32)
    for m in range(2):
        for k in range(4):
            for u in range(2):
                for b in range(4):
                    rows_second[(m * 4 + k) * 8 + u * 4 + b, (2 * b + k) * 4 + 2 * u + m] = 1
    rows_back = np.zeros((32, 96), np.float32)
    for k in range(4):
        for a in range(2, 8):
            for t in range(4):
                r = 2 * a + k - 7
                if 0 <= r < 8:
                    rows_back[t * 8 + r, k * 24 + (a - 2) * 4 + t] = 1
    return (
        jnp.asarray(rows_first, LOW),
        jnp.asarray(rows_second, LOW),
        jnp.asarray(rows_second.T[8:32].copy(), WIDE),
        jnp.asarray(rows_back, WIDE),
    )


def column_sum(left, middle, right):
    column = lax.broadcasted_iota(jnp.int32, middle.shape, 0) % 32
    rows = middle.shape[0]
    return (
        middle
        + jnp.where(column == 0, 0.0, pltpu.roll(left, 1, 0))
        + jnp.where(column == 31, 0.0, pltpu.roll(right, rows - 1, 0))
    )


def across(left, right):
    return lax.dot_general(left, right, (((1,), (1,)), ((), ())), preferred_element_type=WIDE)


def wide_dot(left, right):
    return jnp.dot(left, right, preferred_element_type=WIDE)


def exact_pick(pick, values):
    return jnp.dot(pick, values, precision=lax.Precision.HIGHEST, preferred_element_type=WIDE)


def step_kernel(
    x_hbm, gain1_hbm, w_hbm, gain2_hbm, ow_hbm, d1_hbm, d2_hbm, score_hbm,
    pick_first_hbm, pick_second_hbm, pick_second_back_hbm, pick_first_back_hbm,
    grad_hbm, summed_hbm, scale_ref,
    out_ref, gain1_ref, w_ref, gain2_ref, ow_ref, d1_ref, d2_ref,
    pick_first, pick_second, pick_second_back, pick_first_back,
    xe, ae, ge, mx, ag, wg, xt, g3, w_fwd, w_back,
    ow_f, ow_cols, ow_rows, d1_f, d1_rows, images, sg, sg_flat,
    dw, p1, reach, sums_wide, pair_out, pair_in, plane_out, plane_in, z_out, z_in, z_all, gathered,
    stats, plane, high, load_sem,
    stat_send, stat_recv, halo_send, halo_recv, sum_send, sum_recv,
):
    me = place()
    frame, row, core, y, z_hi = (me["frame"], me["row"], me["core"], me["y"], me["z_hi"])
    z = z_hi * 4 + me["z_lo"]
    slot = frame * 4 + y
    clip_slot = row * 4 + frame
    clip_line = clip_peers(me)
    plane_line, z_line, high_line = (plane_peers(me), z_peers(me), high_peers(me))
    partner = device(me, core=1 - core)
    above, below = (neighbour(me, 0, -1), neighbour(me, 0, 1))

    barrier = pltpu.get_barrier_semaphore()
    greeted = clip_line + [partner] + [
        device(me, z_hi=(z_hi + dz) % 4, z_lo=(me["z_lo"] + dl) % 4)
        for dz in range(4)
        for dl in range(1, 4)
    ]
    for peer in greeted:
        pl.semaphore_signal(
            barrier, inc=1, device_id=peer, device_id_type=pl.DeviceIdType.MESH
        )

    own_strip = (pl.ds(2, 4), pl.ds(1, 8))
    loads = [
        (x_hbm, xe.at[own_strip]),
        (score_hbm, sg.at[:, pl.ds(1, 2)]),
        (w_hbm, w_ref),
        (ow_hbm, ow_ref),
        (d1_hbm, d1_ref),
        (gain1_hbm, gain1_ref),
        (gain2_hbm, gain2_ref),
        (d2_hbm, d2_ref),
        (pick_first_hbm, pick_first),
        (pick_second_hbm, pick_second),
        (pick_second_back_hbm, pick_second_back),
        (pick_first_back_hbm, pick_first_back),
    ]
    loads = [
        pltpu.make_async_copy(src, dst, load_sem.at[index])
        for index, (src, dst) in enumerate(loads)
    ]
    for load in loads:
        load.start()

    def stats_start(turn, first, second, before_nearest=lambda: None):
        stats[turn, clip_slot, 0:1, :] = first
        stats[turn, clip_slot, 1:2, :] = second
        mine = stats.at[turn, clip_slot]
        for index, peer in enumerate(clip_line):
            if index == 48:
                before_nearest()
            push(mine, mine, peer, stat_send.at[turn], stat_recv.at[turn])

    def stats_wait(turn):
        others = stats.at[turn, pl.ds(0, 63)]
        arrived(others, stat_recv.at[turn])

    def moments_end(turn):
        stats_wait(turn)
        parts = stats[turn]
        sums = jnp.sum(parts, axis=0)
        mean = group_total(tile(sums[0:1])) / (4.0 * PER_CLIP)
        apart = parts - mean[0:2]
        spread = jnp.sum(apart * apart, axis=0)
        total = group_total(tile(sums[1:2] + float(LOCAL) * spread[0:1]))
        return (mean[0:1], lax.rsqrt(total[0:1] / (4.0 * LOCAL * PER_CLIP) + EPSILON))

    def sums_end(turn):
        stats_wait(turn)
        sums = jnp.sum(stats[turn], axis=0) / (4.0 * LOCAL * PER_CLIP)
        return (group_total(tile(sums[0:1]))[0:1], group_total(tile(sums[1:2]))[0:1])

    def plane_start(first, second):
        plane[slot, 0:1, :] = first
        plane[slot, 1:2, :] = second
        for _, peer in plane_line:
            push(plane.at[slot], plane.at[slot], peer, stat_send.at[3], stat_recv.at[3])

    def plane_to_high():
        others = plane.at[pl.ds(0, 15)]
        arrived(others, stat_recv.at[3])
        high[z_hi] = jnp.sum(plane[...], axis=0)
        for _, peer in high_line:
            push(high.at[z_hi], high.at[z_hi], peer, stat_send.at[4], stat_recv.at[4])

    def high_end():
        others = high.at[pl.ds(0, 3)]
        arrived(others, stat_recv.at[4])
        sums = jnp.sum(high[...], axis=0) / (4.0 * LOCAL * PER_CLIP)
        return (group_total(tile(sums[0:1]))[0:1], group_total(tile(sums[1:2]))[0:1])

    def local_moments(read):
        zero = jnp.zeros((1, 128), WIDE)
        total = lax.fori_loop(
            0, 4, lambda t, acc: acc + jnp.sum(read(t), axis=0, keepdims=True), zero
        )
        mean = total / float(LOCAL)

        def squares(t, acc):
            apart = read(t) - mean
            return acc + jnp.sum(apart * apart, axis=0, keepdims=True)

        return (mean, lax.fori_loop(0, 4, squares, zero))

    def column_copies(t, values):
        here = pl.ds(t * 256, 256)
        values = values.astype(LOW)
        wide = values.astype(WIDE)
        column = lax.broadcasted_iota(jnp.int32, wide.shape, 0) % 32
        g3[here, 128:256] = values
        g3[here, 0:128] = jnp.where(column == 31, 0.0, pltpu.roll(wide, 255, 0)).astype(LOW)
        g3[here, 256:384] = jnp.where(column == 0, 0.0, pltpu.roll(wide, 1, 0)).astype(LOW)

    def acts_window(i, j):
        return jnp.concatenate([xt[j, i + t] for t in range(4)], axis=1)

    def against_acts(result):
        for i in range(3):
            for j in range(3):
                product = wide_dot(acts_window(i, j), g3[...])
                for c in range(3):
                    first = ((i * 3 + j) * 3 + c) * 128
                    result[first : first + 128, :] = product[:, c * 128 : (c + 1) * 128]

    def halo_start(turn, src, dst, own_row, own_frames, to_frames, frame_step):
        def go(index, source, target, peer):
            push(source, target, peer, halo_send.at[turn, index], halo_recv.at[turn, index])

        inner = pl.ds(own_frames[0], 4)
        edge = pl.ds(own_frames[1], 2)
        base = pl.ds(own_frames[2], 4)
        far = pl.ds(to_frames, 2)
        go(0, src.at[inner, own_row + 7], dst.at[base, 0], below)
        go(1, src.at[inner, own_row], dst.at[base, 9], above)
        go(2, src.at[edge, pl.ds(own_row, 8)], dst.at[far, pl.ds(1, 8)], neighbour(me, frame_step, 0))
        go(3, src.at[edge, own_row + 7], dst.at[far, 0], neighbour(me, frame_step, 1))
        go(4, src.at[edge, own_row], dst.at[far, 9], neighbour(me, frame_step, -1))

    def halo_wait(turn, dst, base_frame, to_frames):
        base = pl.ds(base_frame, 4)
        far = pl.ds(to_frames, 2)
        parts = [
            dst.at[base, 0],
            dst.at[base, 9],
            dst.at[far, pl.ds(1, 8)],
            dst.at[far, 0],
            dst.at[far, 9],
        ]
        for index, part in enumerate(parts):
            arrived(part, halo_recv.at[turn, index])
            arrived(part, halo_send.at[turn, index])

    def inside(shape, outside_frame):
        position = lax.broadcasted_iota(jnp.int32, shape, 0)
        low = jnp.where(row == 0, 32, 0)
        high_end = jnp.where(row == 15, 288, 320)
        high_end = jnp.where(outside_frame, 0, high_end)
        return (position >= low) & (position < high_end)

    def own_input(t):
        return xe[t + 2, 1:9].astype(WIDE).reshape(256, 128)

    loads[0].wait()
    mean, squares = local_moments(own_input)
    loads[1].wait()
    pl.semaphore_wait(barrier, len(greeted))
    stats_start(0, mean, squares, lambda: halo_start(0, xe, xe, 1, (2, 4, 2), 0, 1))
    push(sg.at[:, 2], sg.at[:, 0], below, halo_send.at[0, 5], halo_recv.at[0, 5])
    push(sg.at[:, 1], sg.at[:, 3], above, halo_send.at[0, 6], halo_recv.at[0, 6])
    for load in loads[2:]:
        load.wait()

    @pl.loop(0, 9)
    def _(tap):
        for c in range(3):
            w_fwd[pl.ds(tap * 128, 128), c * 128 : (c + 1) * 128] = w_ref[tap * 3 + c]

    ow_f[...] = jnp.zeros((128, 128), WIDE)
    ow_f[0:3, :] = ow_ref[...].astype(WIDE)
    colours_t = ow_f[...]
    colours = colours_t.T
    for c in range(32):
        ow_cols[c * 128 : (c + 1) * 128, :] = (
            colours if c == 0 else pltpu.roll(colours, 3 * c, 1)
        ).astype(LOW)
        ow_rows[:, c * 128 : (c + 1) * 128] = (
            colours_t if c == 0 else pltpu.roll(colours_t, 3 * c, 0)
        ).astype(LOW)
    for k in range(4):
        d1_f[...] = jnp.zeros((128, 128), WIDE)
        for colour in range(3):
            taps = d1_ref[k * 3 + colour].astype(WIDE)
            for l in range(4):
                d1_f[3 * l + colour : 3 * l + colour + 1, 0:64] = taps[l : l + 1]
        single = d1_f[...]
        double = single + pltpu.roll(pltpu.roll(single, 64, 1), 6, 0)
        for p in range(8):
            d1_rows[k * 128 : (k + 1) * 128, p * 128 : (p + 1) * 128] = pltpu.roll(
                double, (12 * p - 3) % 128, 0
            ).astype(LOW)

    @pl.loop(0, 9)
    def _(tap):
        for c in range(3):
            w_back[pl.ds(tap * 128, 128), c * 128 : (c + 1) * 128] = (
                w_ref[tap * 3 + c].astype(WIDE).T.astype(LOW)
            )

    halo_wait(0, xe, 2, 0)
    for index in (5, 6):
        arrived(sg.at[:, 0], halo_recv.at[0, index])
        arrived(sg.at[:, 0], halo_send.at[0, index])
    gain1 = gain1_ref[...]
    gain2 = gain2_ref[...]
    mean1, inverse1 = moments_end(0)

    @pl.loop(0, 6)
    def _(t):
        scaled = (xe[t].astype(WIDE).reshape(320, 128) - mean1) * inverse1 * gain1
        act = scaled * jax.nn.sigmoid(scaled)
        keep = inside(act.shape, (t < 2) & (frame == 0))
        ae[t] = jnp.where(keep, act, 0.0).astype(LOW).reshape(10, 32, 128)

    @pl.loop(0, 4)
    def _(t):
        taps = [ae[t + i, j : j + 8].reshape(256, 128) for i in range(3) for j in range(3)]
        product = wide_dot(jnp.concatenate(taps, axis=1), w_fwd[...])
        branch = column_sum(product[:, 0:128], product[:, 128:256], product[:, 256:384])
        mx[t] = (xe[t + 2, 1:9].astype(WIDE).reshape(256, 128) + branch).astype(LOW)

    mean, squares = local_moments(lambda t: mx[t].astype(WIDE))
    stats_start(1, mean, squares)

    @pl.loop(0, 6)
    def _(t):
        for j in range(3):
            xt[j, t] = ae[t, j : j + 8].reshape(256, 128).astype(WIDE).T.astype(LOW)

    column = lax.broadcasted_iota(jnp.int32, (1024, 128), 0) % 32
    tap_lane = lax.broadcasted_iota(jnp.int32, (1024, 128), 1)
    reached = ((tap_lane != 0) | (column < 31)) & ((tap_lane != 2) | (column > 0))
    reached = jnp.where(reached, 1.0, 0.0).astype(LOW)
    for i in range(3):
        for j in range(3):
            reach[i * 3 + j] = wide_dot(acts_window(i, j), reached)

    mean2, inverse2 = moments_end(1)

    def normed_second(t):
        return (mx[t].astype(WIDE) - mean2) * inverse2

    @pl.loop(0, 4)
    def _(t):
        scaled = normed_second(t) * gain2
        act = (scaled * jax.nn.sigmoid(scaled)).astype(LOW)
        ag[pl.ds(t * 256, 256), :] = act.astype(WIDE)

    image = jnp.zeros((32, 128), WIDE)
    for part in range(4):
        columns = [ag[pl.ds(c, 32, stride=32), :] for c in range(part * 8, part * 8 + 8)]
        image = image + wide_dot(
            jnp.concatenate(columns, axis=1).astype(LOW), ow_cols[part * 1024 : (part + 1) * 1024, :]
        )
    images[1] = image.astype(LOW)
    push(images.at[1], images.at[0], below, halo_send.at[1, 5], halo_recv.at[1, 5])
    push(images.at[1], images.at[2], above, halo_send.at[1, 6], halo_recv.at[1, 6])

    @pl.loop(0, 4)
    def _(t):
        column_copies(t, normed_second(t))

    against_acts(p1)
    sg_flat[...] = sg[...].reshape(64, 128)
    score = jnp.concatenate([sg_flat[pl.ds(p, 8, stride=8), :] for p in range(8)], axis=0)
    for index in (5, 6):
        arrived(images.at[0], halo_recv.at[1, index])
        arrived(images.at[0], halo_send.at[1, index])

    strips = jnp.concatenate(
        [
            jnp.where(row == 0, 0.0, images[0].astype(WIDE)),
            images[1].astype(WIDE),
            jnp.where(row == 15, 0.0, images[2].astype(WIDE)),
        ],
        axis=0,
    ).astype(LOW)
    picked = wide_dot(pick_first[...], strips)
    taps = [picked[k * 40 : (k + 1) * 40] for k in range(4)]
    first_pre = wide_dot(jnp.concatenate(taps, axis=1).astype(LOW), d1_rows[...])
    place_row = lax.broadcasted_iota(jnp.int32, first_pre.shape, 0)
    low_row = jnp.where(row == 0, 12, 0)
    high_row = jnp.where(row == 15, 28, 40)
    real = (place_row >= low_row) & (place_row < high_row)
    first_act = jnp.where(real, first_pre * jax.nn.sigmoid(first_pre), 0.0).astype(LOW)
    picked = wide_dot(pick_second[...], first_act)
    blank = jnp.zeros((8, 128), WIDE)
    lane = lax.broadcasted_iota(jnp.int32, (64, 128), 1)
    second_pre = jnp.zeros((64, 128), WIDE)
    for tap in range(8):
        middle = jnp.concatenate(
            [picked[tap * 8 : tap * 8 + 8, p * 128 : (p + 1) * 128] for p in range(8)], axis=0
        )
        turned = pltpu.roll(middle, 64, 1)
        sides = jnp.where(
            lane < 64,
            jnp.concatenate([blank, turned[0:56]], axis=0),
            jnp.concatenate([turned[8:64], blank], axis=0),
        )
        weights = jnp.concatenate([d2_ref[tap * 4 + l] for l in (1, 2, 0, 3)], axis=0)
        second_pre = second_pre + wide_dot(
            jnp.concatenate([middle, sides], axis=1).astype(LOW), weights
        )
    strip = lax.broadcasted_iota(jnp.int32, (64, 128), 0) % 4
    first_strip = jnp.where(row == 0, 1, 0)
    last_strip = jnp.where(row == 15, 2, 3)
    score_pre = jnp.where(
        (strip >= first_strip) & (strip <= last_strip), score * silu_slope(second_pre), 0.0
    ).astype(LOW).astype(WIDE)
    sources = jnp.concatenate(
        [
            score_pre,
            jnp.concatenate([blank, score_pre[0:56]], axis=0),
            jnp.concatenate([score_pre[8:64], blank], axis=0),
        ],
        axis=1,
    ).astype(LOW)
    nothing = jnp.zeros((64, 128), LOW)
    spread = []
    for tap in range(8):
        even = jnp.concatenate([d2_ref[tap * 4 + 1], d2_ref[tap * 4 + 3], nothing], axis=1)
        odd = jnp.concatenate([d2_ref[tap * 4 + 2], nothing, d2_ref[tap * 4]], axis=1)
        back = across(sources, jnp.concatenate([even, odd], axis=0))
        spread.append(
            jnp.concatenate([back[p * 8 : (p + 1) * 8] for p in range(8)], axis=1)
        )
    first_full = exact_pick(pick_second_back[...], jnp.concatenate(spread, axis=0))
    first_grad = jnp.where(real[8:32], first_full * silu_slope(first_pre[8:32]), 0.0).astype(LOW)
    back = across(first_grad, d1_rows[...])
    stacked = jnp.concatenate([back[:, k * 128 : (k + 1) * 128] for k in range(4)], axis=0)
    image_grad = exact_pick(pick_first_back[...], stacked).astype(LOW)
    for part in range(4):
        grads = wide_dot(image_grad, ow_rows[:, part * 1024 : (part + 1) * 1024])
        for c in range(8):
            ag[pl.ds(part * 8 + c, 32, stride=32), :] = grads[:, c * 128 : (c + 1) * 128]

    def weigh(t, acc):
        normed = normed_second(t)
        here = pl.ds(t * 256, 256)
        weighted = ag[here, :] * silu_slope(normed * gain2) * gain2
        ag[here, :] = weighted
        column_copies(t, weighted * inverse2)
        return (
            acc[0] + jnp.sum(weighted, axis=0, keepdims=True),
            acc[1] + jnp.sum(weighted * normed, axis=0, keepdims=True),
        )

    zeros = (jnp.zeros((1, 128), WIDE), jnp.zeros((1, 128), WIDE))
    sums = lax.fori_loop(0, 4, weigh, zeros)
    stats_start(2, *sums)
    against_acts(dw)
    for i in range(9):
        for c in range(3):
            first = (i * 3 + c) * 128
            sums_wide[first : first + 128, :] = jnp.broadcast_to(reach[i, :, c : c + 1], (128, 128))
    for array in (dw, p1, sums_wide):
        array[3456:3520, :] = jnp.zeros((64, 128), WIDE)
    first_mean, second_mean = sums_end(2)

    first_part, second_part = (first_mean * inverse2, second_mean * inverse2)
    theirs = pl.ds(pl.multiple_of((1 - core) * 1728, 64), 1792)
    ours = pl.ds(pl.multiple_of(core * 1728, 64), 1792)
    chunks = (pl.ds(0, 64), pl.ds(64, 48))

    def corrected(rows):
        return dw[rows, :] - sums_wide[rows, :] * first_part - p1[rows, :] * second_part

    pair_out[...] = corrected(theirs).astype(LOW).reshape(16, 112, 128)
    for turn, chunk in enumerate(chunks):
        push(pair_out.at[:, chunk], pair_in.at[:, chunk], partner, sum_send.at[turn], sum_recv.at[turn])

    @pl.loop(0, 4)
    def _(t):
        here = pl.ds(t * 256, 256)
        grad = (ag[here, :] - first_mean - normed_second(t) * second_mean) * inverse2
        ag[here, :] = grad
        ge[t, 1:9] = grad.astype(LOW).reshape(8, 32, 128)

    halo_start(1, ge, ge, 1, (0, 0, 0), 4, -1)

    dw[ours, :] = corrected(ours)
    for turn, chunk in enumerate(chunks):
        arrived(pair_in.at[:, chunk], sum_recv.at[turn])
        mine = dw[ours, :].reshape(16, 112, 128)[:, chunk.start : chunk.start + chunk.size]
        plane_out[:, chunk] = (mine + pair_in[:, chunk].astype(WIDE)).astype(LOW)
        for other, peer in plane_line:
            push(
                plane_out.at[other, chunk],
                plane_in.at[slot, chunk],
                peer,
                sum_send.at[2 + turn],
                sum_recv.at[2 + turn],
            )
        plane_in[slot, chunk] = plane_out[slot, chunk]

    tiles = (range(0, 4), range(4, 7))
    own_tile = z % 8
    owns = (own_tile < 4, (own_tile >= 4) & (own_tile < 7))
    for turn, chunk in enumerate(chunks):
        others = plane_in.at[pl.ds(0, 15), chunk]
        arrived(others, sum_recv.at[2 + turn])
        total = jnp.sum(plane_in[:, chunk].astype(WIDE), axis=0).astype(LOW)
        for index, part in enumerate(tiles[turn]):
            z_out[part] = total[index * 16 : (index + 1) * 16]
            for owner in (part, part + 8):

                @pl.when(z != owner)
                def _():
                    push(
                        z_out.at[part],
                        z_in.at[z],
                        device(me, z_hi=owner // 4, z_lo=owner % 4),
                        sum_send.at[4 + turn],
                        sum_recv.at[4],
                    )

    halo_wait(1, ge, 0, 4)

    def normed_first(t):
        return (own_input(t) - mean1) * inverse1

    def back_step(t, acc):
        taps = []
        for i in range(3):
            for j in range(3):
                strip = ge[t + 2 - i, 2 - j : 10 - j].reshape(256, 128)
                above_edge = (row == 0) if j == 2 else False
                below_edge = (row == 15) if j == 0 else False
                late = (frame == 3) & (t + 2 - i > 3)
                position = lax.broadcasted_iota(jnp.int32, (256, 128), 0)
                low = jnp.where(above_edge, 32, 0)
                end = jnp.where(late, 0, jnp.where(below_edge, 224, 256))
                keep = (position >= low) & (position < end)
                taps.append(jnp.where(keep, strip.astype(WIDE), 0.0).astype(LOW))
        product = wide_dot(jnp.concatenate(taps, axis=1), w_back[...])
        grad = column_sum(product[:, 256:384], product[:, 128:256], product[:, 0:128])
        normed = normed_first(t)
        weighted = grad * silu_slope(normed * gain1) * gain1
        wg[t] = weighted
        return (
            acc[0] + jnp.sum(weighted, axis=0, keepdims=True),
            acc[1] + jnp.sum(weighted * normed, axis=0, keepdims=True),
        )

    sums = lax.fori_loop(0, 4, back_step, zeros)
    plane_start(*sums)

    for turn in range(2):

        @pl.when(owns[turn])
        def _():
            z_in[z] = z_out[own_tile]
            arrived(z_in.at[pl.ds(0, 15)], sum_recv.at[4])
            z_all[own_tile] = jnp.sum(z_in[...].astype(WIDE), axis=0).astype(LOW)
            mine = z_all.at[own_tile]
            for step in (-4, 3, -3, 2, -2, 1, -1):
                other = (z + step) % 16
                peer = device(me, z_hi=other // 4, z_lo=other % 4)
                push(mine, mine, peer, sum_send.at[6], sum_recv.at[6 + turn])

    plane_to_high()

    half, other_half = (gathered.at[core], gathered.at[1 - core])
    for turn, chunk in enumerate(chunks):
        count = len(tiles[turn])

        @pl.when(owns[turn])
        def _():
            arrived(z_all.at[pl.ds(0, count - 1)], sum_recv.at[6 + turn])

        @pl.when(jnp.logical_not(owns[turn]))
        def _():
            arrived(z_all.at[pl.ds(0, count)], sum_recv.at[6 + turn])

        first = tiles[turn].start
        half[slot, chunk] = z_all[first : first + count].reshape(count * 16, 128)
        for _, peer in plane_line:
            push(
                half.at[slot, chunk],
                half.at[slot, chunk],
                peer,
                sum_send.at[8 + turn],
                sum_recv.at[8 + turn],
            )

    first_mean, second_mean = high_end()

    @pl.loop(0, 4)
    def _(t):
        grad = (wg[t] - first_mean - normed_first(t) * second_mean) * inverse1
        out_ref[t] = (ag[pl.ds(t * 256, 256), :] + grad).astype(LOW).reshape(8, 32, 128)

    out_copy = pltpu.make_async_copy(out_ref, grad_hbm, load_sem.at[12])
    out_copy.start()

    def squares_of(part_of, chunk):
        def add(part, acc):
            piece = part_of[part, chunk].astype(WIDE)
            return acc + jnp.sum((piece * piece).reshape(chunk.size // 8, 8, 128), axis=0)

        total = lax.fori_loop(0, 15, add, jnp.zeros((8, 128), WIDE))
        if chunk.start == 0:
            piece = part_of[15, 0:48].astype(WIDE)
            total = total + jnp.sum((piece * piece).reshape(6, 8, 128), axis=0)
        return total

    squares = []
    for turn, chunk in enumerate(chunks):
        others = half.at[pl.ds(0, 15), chunk]
        arrived(others, sum_recv.at[8 + turn])
        push(half.at[:, chunk], half.at[:, chunk], partner, sum_send.at[10 + turn], sum_recv.at[10 + turn])
        squares.append(squares_of(half, chunk))
    own_copy = pltpu.make_async_copy(half, summed_hbm.at[core], load_sem.at[13])
    own_copy.start()
    for turn, chunk in enumerate(chunks):
        arrived(other_half.at[:, chunk], sum_recv.at[10 + turn])
    other_copy = pltpu.make_async_copy(other_half, summed_hbm.at[1 - core], load_sem.at[14])
    other_copy.start()
    for chunk in chunks:
        squares.append(squares_of(other_half, chunk))
    total = (squares[0] + squares[1]) + (squares[2] + squares[3])
    mean = jnp.sum(total, keepdims=True) / (3456.0 * 128.0)
    scale_ref[...] = jnp.broadcast_to(lax.rsqrt(mean + EPSILON), (8, 128))

    for turn in range(3):
        arrived(stats.at[turn, pl.ds(0, 63)], stat_send.at[turn])
    arrived(plane.at[pl.ds(0, 15)], stat_send.at[3])
    arrived(high.at[pl.ds(0, 3)], stat_send.at[4])
    for turn, chunk in enumerate(chunks):
        count = len(tiles[turn])
        arrived(pair_in.at[:, chunk], sum_send.at[turn])
        arrived(plane_in.at[pl.ds(0, 15), chunk], sum_send.at[2 + turn])
        arrived(half.at[pl.ds(0, 15), chunk], sum_send.at[8 + turn])
        arrived(half.at[:, chunk], sum_send.at[10 + turn])

        @pl.when(owns[turn])
        def _():
            arrived(z_in.at[pl.ds(0, 2 * count - 1)], sum_send.at[4 + turn])
            arrived(z_in.at[pl.ds(0, 7)], sum_send.at[6])

        @pl.when(jnp.logical_not(owns[turn]))
        def _():
            arrived(z_in.at[pl.ds(0, 2 * count)], sum_send.at[4 + turn])

    for copy in (out_copy, own_copy, other_copy):
        copy.wait()


def finish_kernel(grad_ref, summed_ref, scale_ref, out_ref, upd_ref):
    out_ref[...] = grad_ref[...]
    scale = scale_ref[0:1, :]
    values = summed_ref[0, 0:15].reshape(1680, 128)
    upd_ref[0, 0:1680, :] = values.astype(WIDE) * scale
    upd_ref[0, 1680:1728, :] = summed_ref[0, 15, 0:48].astype(WIDE) * scale


def shards(
    block_input, gain_first, conv_weight, gain_second, out_weight, disc_first, disc_second, score_grad
):
    vmem = pl.BlockSpec(memory_space=pltpu.VMEM)
    low = lambda *shape: pltpu.VMEM(shape, LOW)
    wide = lambda *shape: pltpu.VMEM(shape, WIDE)
    dma = pltpu.SemaphoreType.DMA
    picks = selections()
    hbm = pl.BlockSpec(memory_space=pltpu.HBM)
    input_grad, summed, scale = pl.pallas_call(
        step_kernel,
        out_shape=(
            jax.ShapeDtypeStruct((4, 8, 32, 128), LOW),
            jax.ShapeDtypeStruct((2, 16, 112, 128), LOW),
            jax.ShapeDtypeStruct((8, 128), WIDE),
        ),
        in_specs=[hbm] * 12,
        out_specs=(hbm, hbm, vmem),
        scratch_shapes=[
            low(4, 8, 32, 128), wide(1, 128), low(27, 128, 128), wide(1, 128), low(3, 128), low(12, 4, 64),
            low(32, 64, 128), low(160, 96), low(64, 40), wide(24, 64), wide(32, 96),
            low(6, 10, 32, 128), low(6, 10, 32, 128), low(6, 10, 32, 128),
            low(4, 256, 128), wide(1024, 128), wide(4, 256, 128),
            low(3, 6, 128, 256), low(1024, 384), low(1152, 384), low(1152, 384),
            wide(128, 128), low(4096, 128), low(128, 4096), wide(128, 128), low(512, 1024),
            low(3, 32, 128), wide(2, 4, 8, 128), wide(64, 128),
            wide(3520, 128), wide(3520, 128), wide(9, 128, 128), wide(3520, 128), low(16, 112, 128), low(16, 112, 128), low(16, 112, 128), low(16, 112, 128),
            low(7, 16, 128), low(16, 16, 128), low(7, 16, 128), low(2, 16, 112, 128),
            wide(3, 64, 2, 128), wide(16, 2, 128), wide(4, 2, 128),
            dma((15,)), dma((5,)), dma((5,)), dma((2, 7)), dma((2, 7)), dma((12,)), dma((12,)),
        ],
        compiler_params=pltpu.CompilerParams(
            collective_id=1, has_side_effects=True, vmem_limit_bytes=64 * 1024 * 1024
        ),
    )(
        block_input[0],
        gain_first.reshape(1, 128),
        conv_weight.reshape(27, 128, 128),
        gain_second.reshape(1, 128),
        out_weight.T,
        disc_first[0].transpose(0, 2, 1, 3).reshape(12, 4, 64),
        disc_second.reshape(32, 64, 128),
        score_grad[0],
        *picks,
    )
    input_grad, update = pl.pallas_call(
        finish_kernel,
        out_shape=(
            jax.ShapeDtypeStruct((4, 8, 32, 128), LOW),
            jax.ShapeDtypeStruct((2, 1728, 128), WIDE),
        ),
        grid=(2,),
        in_specs=[
            pl.BlockSpec((2, 8, 32, 128), lambda half: (half, 0, 0, 0)),
            pl.BlockSpec((1, 16, 112, 128), lambda half: (half, 0, 0, 0)),
            pl.BlockSpec((8, 128), lambda half: (0, 0)),
        ],
        out_specs=(
            pl.BlockSpec((2, 8, 32, 128), lambda half: (half, 0, 0, 0)),
            pl.BlockSpec((1, 1728, 128), lambda half: (half, 0, 0)),
        ),
        compiler_params=pltpu.CompilerParams(vmem_limit_bytes=64 * 1024 * 1024),
    )(input_grad, summed, scale)
    return (input_grad[None], update.reshape(conv_weight.shape))


def solution(mesh):
    split = P("batch", "frame", "row", None, None)
    in_specs = (split, P(), P(), P(), P(), P(), P(), split)
    return jax.shard_map(
        shards, mesh=mesh, in_specs=in_specs, out_specs=(split, P()), check_vma=False
    )
```

```python
import jax
import jax.numpy as jnp
import numpy as np
from jax import lax
from jax.experimental import pallas as pl
from jax.experimental.pallas import tpu as pltpu
from jax.sharding import PartitionSpec as P

EPSILON = 1e-06
LOW = jnp.bfloat16
WIDE = jnp.float32
LOCAL = 1024
PER_CLIP = 64


def group_total(values):
    lane = lax.broadcasted_iota(jnp.int32, values.shape, 1)
    paired = values + jnp.where(
        lane % 2 == 0, pltpu.roll(values, 127, 1), pltpu.roll(values, 1, 1)
    )
    return paired + jnp.where(
        lane % 4 < 2, pltpu.roll(paired, 126, 1), pltpu.roll(paired, 2, 1)
    )


def tile(row):
    return jnp.broadcast_to(row, (8, row.shape[-1]))


def silu_slope(values):
    logistic = jax.nn.sigmoid(values)
    return logistic * (1.0 + values * (1.0 - logistic))


def place():
    batch = lax.axis_index("batch")
    row = lax.axis_index("row")
    return dict(
        batch=batch,
        z_lo=batch // 2,
        core=batch % 2,
        frame=lax.axis_index("frame"),
        row=row,
        z_hi=row // 4,
        y=row % 4,
    )


def device(me, **changed):
    at = dict(me, **changed)
    return (at["z_lo"] * 2 + at["core"], at["frame"], at["z_hi"] * 4 + at["y"])


def neighbour(me, frame_step, row_step):
    return (me["batch"], (me["frame"] + frame_step) % 4, (me["row"] + row_step) % 16)


def plane_peers(me):
    own = me["frame"] * 4 + me["y"]
    others = [(own + step) % 16 for step in range(1, 16)]
    return [(other, device(me, frame=other // 4, y=other % 4)) for other in others]


def z_peers(me):
    own = me["z_hi"] * 4 + me["z_lo"]
    others = [(own + step) % 16 for step in range(1, 16)]
    return [(other, device(me, z_hi=other // 4, z_lo=other % 4)) for other in others]


def clip_peers(me):
    return [
        device(
            me,
            z_hi=(me["z_hi"] + dz) % 4,
            y=(me["y"] + dy) % 4,
            frame=(me["frame"] + dx) % 4,
        )
        for dz in (2, 1, 3, 0)
        for dy in (2, 1, 3, 0)
        for dx in (2, 1, 3, 0)
        if (dz, dy, dx) != (0, 0, 0)
    ]


def high_peers(me):
    others = [(me["z_hi"] + step) % 4 for step in range(1, 4)]
    return [(other, device(me, z_hi=other)) for other in others]


def push(src, dst, peer, send_sem, recv_sem):
    pltpu.make_async_remote_copy(
        src_ref=src,
        dst_ref=dst,
        send_sem=send_sem,
        recv_sem=recv_sem,
        device_id=peer,
        device_id_type=pl.DeviceIdType.MESH,
    ).start()


def arrived(like, sem):
    pltpu.make_async_copy(like, like, sem).wait()


def selections():
    rows_first = np.zeros((160, 96), np.float32)
    for k in range(4):
        for a in range(10):
            for t in range(4):
                block, r = divmod(2 * a + k + 1, 8)
                rows_first[k * 40 + a * 4 + t, block * 32 + t * 8 + r] = 1
    rows_second = np.zeros((64, 40), np.float32)
    for m in range(2):
        for k in range(4):
            for u in range(2):
                for b in range(4):
                    rows_second[(m * 4 + k) * 8 + u * 4 + b, (2 * b + k) * 4 + 2 * u + m] = 1
    rows_back = np.zeros((32, 96), np.float32)
    for k in range(4):
        for a in range(2, 8):
            for t in range(4):
                r = 2 * a + k - 7
                if 0 <= r < 8:
                    rows_back[t * 8 + r, k * 24 + (a - 2) * 4 + t] = 1
    return (
        jnp.asarray(rows_first, LOW),
        jnp.asarray(rows_second, LOW),
        jnp.asarray(rows_second.T[8:32].copy(), WIDE),
        jnp.asarray(rows_back, WIDE),
    )


def column_sum(left, middle, right):
    column = lax.broadcasted_iota(jnp.int32, middle.shape, 0) % 32
    rows = middle.shape[0]
    return (
        middle
        + jnp.where(column == 0, 0.0, pltpu.roll(left, 1, 0))
        + jnp.where(column == 31, 0.0, pltpu.roll(right, rows - 1, 0))
    )


def across(left, right):
    return lax.dot_general(left, right, (((1,), (1,)), ((), ())), preferred_element_type=WIDE)


def wide_dot(left, right):
    return jnp.dot(left, right, preferred_element_type=WIDE)


def exact_pick(pick, values):
    return jnp.dot(pick, values, precision=lax.Precision.HIGHEST, preferred_element_type=WIDE)


def step_kernel(
    x_hbm, gain1_hbm, w_hbm, gain2_hbm, ow_hbm, d1_hbm, d2_hbm, score_hbm,
    pick_first_hbm, pick_second_hbm, pick_second_back_hbm, pick_first_back_hbm,
    grad_hbm, summed_hbm, scale_ref,
    out_ref, gain1_ref, w_ref, gain2_ref, ow_ref, d1_ref, d2_ref,
    pick_first, pick_second, pick_second_back, pick_first_back,
    xe, ae, ge, mx, ag, wg, xt, g3, w_fwd, w_back,
    ow_f, ow_cols, ow_rows, d1_f, d1_rows, images, sg, sg_flat,
    dw, p1, reach, sums_wide, pair_out, pair_in, plane_out, plane_in, z_out, z_in, z_all, gathered,
    stats, plane, high, load_sem,
    stat_send, stat_recv, halo_send, halo_recv, sum_send, sum_recv,
):
    me = place()
    frame, row, core, y, z_hi = (me["frame"], me["row"], me["core"], me["y"], me["z_hi"])
    z = z_hi * 4 + me["z_lo"]
    slot = frame * 4 + y
    clip_slot = row * 4 + frame
    clip_line = clip_peers(me)
    plane_line, z_line, high_line = (plane_peers(me), z_peers(me), high_peers(me))
    partner = device(me, core=1 - core)
    above, below = (neighbour(me, 0, -1), neighbour(me, 0, 1))

    barrier = pltpu.get_barrier_semaphore()
    greeted = clip_line + [partner] + [
        device(me, z_hi=(z_hi + dz) % 4, z_lo=(me["z_lo"] + dl) % 4)
        for dz in range(4)
        for dl in range(1, 4)
    ]
    for peer in greeted:
        pl.semaphore_signal(
            barrier, inc=1, device_id=peer, device_id_type=pl.DeviceIdType.MESH
        )

    own_strip = (pl.ds(2, 4), pl.ds(1, 8))
    loads = [
        (x_hbm, xe.at[own_strip]),
        (score_hbm, sg.at[:, pl.ds(1, 2)]),
        (w_hbm, w_ref),
        (ow_hbm, ow_ref),
        (d1_hbm, d1_ref),
        (gain1_hbm, gain1_ref),
        (gain2_hbm, gain2_ref),
        (d2_hbm, d2_ref),
        (pick_first_hbm, pick_first),
        (pick_second_hbm, pick_second),
        (pick_second_back_hbm, pick_second_back),
        (pick_first_back_hbm, pick_first_back),
    ]
    loads = [
        pltpu.make_async_copy(src, dst, load_sem.at[index])
        for index, (src, dst) in enumerate(loads)
    ]
    for load in loads:
        load.start()

    def stats_start(turn, first, second, after_farthest=lambda: None):
        stats[turn, clip_slot, 0:1, :] = first
        stats[turn, clip_slot, 1:2, :] = second
        mine = stats.at[turn, clip_slot]
        for index, peer in enumerate(clip_line):
            if index == 16:
                after_farthest()
            push(mine, mine, peer, stat_send.at[turn], stat_recv.at[turn])

    def stats_wait(turn):
        others = stats.at[turn, pl.ds(0, 63)]
        arrived(others, stat_recv.at[turn])

    def moments_end(turn):
        stats_wait(turn)
        parts = stats[turn]
        sums = jnp.sum(parts, axis=0)
        mean = group_total(tile(sums[0:1])) / (4.0 * PER_CLIP)
        apart = parts - mean[0:2]
        spread = jnp.sum(apart * apart, axis=0)
        total = group_total(tile(sums[1:2] + float(LOCAL) * spread[0:1]))
        return (mean[0:1], lax.rsqrt(total[0:1] / (4.0 * LOCAL * PER_CLIP) + EPSILON))

    def sums_end(turn):
        stats_wait(turn)
        sums = jnp.sum(stats[turn], axis=0) / (4.0 * LOCAL * PER_CLIP)
        return (group_total(tile(sums[0:1]))[0:1], group_total(tile(sums[1:2]))[0:1])

    def plane_start(first, second):
        plane[slot, 0:1, :] = first
        plane[slot, 1:2, :] = second
        for _, peer in plane_line:
            push(plane.at[slot], plane.at[slot], peer, stat_send.at[3], stat_recv.at[3])

    def plane_to_high():
        others = plane.at[pl.ds(0, 15)]
        arrived(others, stat_recv.at[3])
        high[z_hi] = jnp.sum(plane[...], axis=0)
        for _, peer in high_line:
            push(high.at[z_hi], high.at[z_hi], peer, stat_send.at[4], stat_recv.at[4])

    def high_end():
        others = high.at[pl.ds(0, 3)]
        arrived(others, stat_recv.at[4])
        sums = jnp.sum(high[...], axis=0) / (4.0 * LOCAL * PER_CLIP)
        return (group_total(tile(sums[0:1]))[0:1], group_total(tile(sums[1:2]))[0:1])

    def local_moments(read):
        zero = jnp.zeros((1, 128), WIDE)
        total = lax.fori_loop(
            0, 4, lambda t, acc: acc + jnp.sum(read(t), axis=0, keepdims=True), zero
        )
        mean = total / float(LOCAL)

        def squares(t, acc):
            apart = read(t) - mean
            return acc + jnp.sum(apart * apart, axis=0, keepdims=True)

        return (mean, lax.fori_loop(0, 4, squares, zero))

    def column_copies(t, values):
        here = pl.ds(t * 256, 256)
        values = values.astype(LOW)
        wide = values.astype(WIDE)
        column = lax.broadcasted_iota(jnp.int32, wide.shape, 0) % 32
        g3[here, 128:256] = values
        g3[here, 0:128] = jnp.where(column == 31, 0.0, pltpu.roll(wide, 255, 0)).astype(LOW)
        g3[here, 256:384] = jnp.where(column == 0, 0.0, pltpu.roll(wide, 1, 0)).astype(LOW)

    def acts_window(i, j):
        return jnp.concatenate([xt[j, i + t] for t in range(4)], axis=1)

    def against_acts(result):
        for i in range(3):
            for j in range(3):
                product = wide_dot(acts_window(i, j), g3[...])
                for c in range(3):
                    first = ((i * 3 + j) * 3 + c) * 128
                    result[first : first + 128, :] = product[:, c * 128 : (c + 1) * 128]

    def halo_start(turn, src, dst, own_row, own_frames, to_frames, frame_step):
        def go(index, source, target, peer):
            push(source, target, peer, halo_send.at[turn, index], halo_recv.at[turn, index])

        inner = pl.ds(own_frames[0], 4)
        edge = pl.ds(own_frames[1], 2)
        base = pl.ds(own_frames[2], 4)
        far = pl.ds(to_frames, 2)
        go(0, src.at[inner, own_row + 7], dst.at[base, 0], below)
        go(1, src.at[inner, own_row], dst.at[base, 9], above)
        go(2, src.at[edge, pl.ds(own_row, 8)], dst.at[far, pl.ds(1, 8)], neighbour(me, frame_step, 0))
        go(3, src.at[edge, own_row + 7], dst.at[far, 0], neighbour(me, frame_step, 1))
        go(4, src.at[edge, own_row], dst.at[far, 9], neighbour(me, frame_step, -1))

    def halo_wait(turn, dst, base_frame, to_frames):
        base = pl.ds(base_frame, 4)
        far = pl.ds(to_frames, 2)
        parts = [
            dst.at[base, 0],
            dst.at[base, 9],
            dst.at[far, pl.ds(1, 8)],
            dst.at[far, 0],
            dst.at[far, 9],
        ]
        for index, part in enumerate(parts):
            arrived(part, halo_recv.at[turn, index])
            arrived(part, halo_send.at[turn, index])

    def inside(shape, outside_frame):
        position = lax.broadcasted_iota(jnp.int32, shape, 0)
        low = jnp.where(row == 0, 32, 0)
        high_end = jnp.where(row == 15, 288, 320)
        high_end = jnp.where(outside_frame, 0, high_end)
        return (position >= low) & (position < high_end)

    def own_input(t):
        return xe[t + 2, 1:9].astype(WIDE).reshape(256, 128)

    loads[0].wait()
    mean, squares = local_moments(own_input)
    loads[1].wait()
    pl.semaphore_wait(barrier, len(greeted))
    stats_start(0, mean, squares, lambda: halo_start(0, xe, xe, 1, (2, 4, 2), 0, 1))
    push(sg.at[:, 2], sg.at[:, 0], below, halo_send.at[0, 5], halo_recv.at[0, 5])
    push(sg.at[:, 1], sg.at[:, 3], above, halo_send.at[0, 6], halo_recv.at[0, 6])
    for load in loads[2:]:
        load.wait()

    @pl.loop(0, 9)
    def _(tap):
        for c in range(3):
            w_fwd[pl.ds(tap * 128, 128), c * 128 : (c + 1) * 128] = w_ref[tap * 3 + c]

    ow_f[...] = jnp.zeros((128, 128), WIDE)
    ow_f[0:3, :] = ow_ref[...].astype(WIDE)
    colours_t = ow_f[...]
    colours = colours_t.T
    for c in range(32):
        ow_cols[c * 128 : (c + 1) * 128, :] = (
            colours if c == 0 else pltpu.roll(colours, 3 * c, 1)
        ).astype(LOW)
        ow_rows[:, c * 128 : (c + 1) * 128] = (
            colours_t if c == 0 else pltpu.roll(colours_t, 3 * c, 0)
        ).astype(LOW)
    for k in range(4):
        d1_f[...] = jnp.zeros((128, 128), WIDE)
        for colour in range(3):
            taps = d1_ref[k * 3 + colour].astype(WIDE)
            for l in range(4):
                d1_f[3 * l + colour : 3 * l + colour + 1, 0:64] = taps[l : l + 1]
        single = d1_f[...]
        double = single + pltpu.roll(pltpu.roll(single, 64, 1), 6, 0)
        for p in range(8):
            d1_rows[k * 128 : (k + 1) * 128, p * 128 : (p + 1) * 128] = pltpu.roll(
                double, (12 * p - 3) % 128, 0
            ).astype(LOW)

    @pl.loop(0, 9)
    def _(tap):
        for c in range(3):
            w_back[pl.ds(tap * 128, 128), c * 128 : (c + 1) * 128] = (
                w_ref[tap * 3 + c].astype(WIDE).T.astype(LOW)
            )

    halo_wait(0, xe, 2, 0)
    for index in (5, 6):
        arrived(sg.at[:, 0], halo_recv.at[0, index])
        arrived(sg.at[:, 0], halo_send.at[0, index])
    gain1 = gain1_ref[...]
    gain2 = gain2_ref[...]
    mean1, inverse1 = moments_end(0)

    @pl.loop(0, 6)
    def _(t):
        scaled = (xe[t].astype(WIDE).reshape(320, 128) - mean1) * inverse1 * gain1
        act = scaled * jax.nn.sigmoid(scaled)
        keep = inside(act.shape, (t < 2) & (frame == 0))
        ae[t] = jnp.where(keep, act, 0.0).astype(LOW).reshape(10, 32, 128)

    @pl.loop(0, 4)
    def _(t):
        taps = [ae[t + i, j : j + 8].reshape(256, 128) for i in range(3) for j in range(3)]
        product = wide_dot(jnp.concatenate(taps, axis=1), w_fwd[...])
        branch = column_sum(product[:, 0:128], product[:, 128:256], product[:, 256:384])
        mx[t] = (xe[t + 2, 1:9].astype(WIDE).reshape(256, 128) + branch).astype(LOW)

    mean, squares = local_moments(lambda t: mx[t].astype(WIDE))
    stats_start(1, mean, squares)

    @pl.loop(0, 6)
    def _(t):
        for j in range(3):
            xt[j, t] = ae[t, j : j + 8].reshape(256, 128).astype(WIDE).T.astype(LOW)

    column = lax.broadcasted_iota(jnp.int32, (1024, 128), 0) % 32
    tap_lane = lax.broadcasted_iota(jnp.int32, (1024, 128), 1)
    reached = ((tap_lane != 0) | (column < 31)) & ((tap_lane != 2) | (column > 0))
    reached = jnp.where(reached, 1.0, 0.0).astype(LOW)
    for i in range(3):
        for j in range(3):
            reach[i * 3 + j] = wide_dot(acts_window(i, j), reached)

    mean2, inverse2 = moments_end(1)

    def normed_second(t):
        return (mx[t].astype(WIDE) - mean2) * inverse2

    @pl.loop(0, 4)
    def _(t):
        scaled = normed_second(t) * gain2
        act = (scaled * jax.nn.sigmoid(scaled)).astype(LOW)
        ag[pl.ds(t * 256, 256), :] = act.astype(WIDE)

    image = jnp.zeros((32, 128), WIDE)
    for part in range(4):
        columns = [ag[pl.ds(c, 32, stride=32), :] for c in range(part * 8, part * 8 + 8)]
        image = image + wide_dot(
            jnp.concatenate(columns, axis=1).astype(LOW), ow_cols[part * 1024 : (part + 1) * 1024, :]
        )
    images[1] = image.astype(LOW)
    push(images.at[1], images.at[0], below, halo_send.at[1, 5], halo_recv.at[1, 5])
    push(images.at[1], images.at[2], above, halo_send.at[1, 6], halo_recv.at[1, 6])

    @pl.loop(0, 4)
    def _(t):
        column_copies(t, normed_second(t))

    against_acts(p1)
    sg_flat[...] = sg[...].reshape(64, 128)
    score = jnp.concatenate([sg_flat[pl.ds(p, 8, stride=8), :] for p in range(8)], axis=0)
    for index in (5, 6):
        arrived(images.at[0], halo_recv.at[1, index])
        arrived(images.at[0], halo_send.at[1, index])

    strips = jnp.concatenate(
        [
            jnp.where(row == 0, 0.0, images[0].astype(WIDE)),
            images[1].astype(WIDE),
            jnp.where(row == 15, 0.0, images[2].astype(WIDE)),
        ],
        axis=0,
    ).astype(LOW)
    picked = wide_dot(pick_first[...], strips)
    taps = [picked[k * 40 : (k + 1) * 40] for k in range(4)]
    first_pre = wide_dot(jnp.concatenate(taps, axis=1).astype(LOW), d1_rows[...])
    place_row = lax.broadcasted_iota(jnp.int32, first_pre.shape, 0)
    low_row = jnp.where(row == 0, 12, 0)
    high_row = jnp.where(row == 15, 28, 40)
    real = (place_row >= low_row) & (place_row < high_row)
    first_act = jnp.where(real, first_pre * jax.nn.sigmoid(first_pre), 0.0).astype(LOW)
    picked = wide_dot(pick_second[...], first_act)
    blank = jnp.zeros((8, 128), WIDE)
    lane = lax.broadcasted_iota(jnp.int32, (64, 128), 1)
    second_pre = jnp.zeros((64, 128), WIDE)
    for tap in range(8):
        middle = jnp.concatenate(
            [picked[tap * 8 : tap * 8 + 8, p * 128 : (p + 1) * 128] for p in range(8)], axis=0
        )
        turned = pltpu.roll(middle, 64, 1)
        sides = jnp.where(
            lane < 64,
            jnp.concatenate([blank, turned[0:56]], axis=0),
            jnp.concatenate([turned[8:64], blank], axis=0),
        )
        weights = jnp.concatenate([d2_ref[tap * 4 + l] for l in (1, 2, 0, 3)], axis=0)
        second_pre = second_pre + wide_dot(
            jnp.concatenate([middle, sides], axis=1).astype(LOW), weights
        )
    strip = lax.broadcasted_iota(jnp.int32, (64, 128), 0) % 4
    first_strip = jnp.where(row == 0, 1, 0)
    last_strip = jnp.where(row == 15, 2, 3)
    score_pre = jnp.where(
        (strip >= first_strip) & (strip <= last_strip), score * silu_slope(second_pre), 0.0
    ).astype(LOW).astype(WIDE)
    sources = jnp.concatenate(
        [
            score_pre,
            jnp.concatenate([blank, score_pre[0:56]], axis=0),
            jnp.concatenate([score_pre[8:64], blank], axis=0),
        ],
        axis=1,
    ).astype(LOW)
    nothing = jnp.zeros((64, 128), LOW)
    spread = []
    for tap in range(8):
        even = jnp.concatenate([d2_ref[tap * 4 + 1], d2_ref[tap * 4 + 3], nothing], axis=1)
        odd = jnp.concatenate([d2_ref[tap * 4 + 2], nothing, d2_ref[tap * 4]], axis=1)
        back = across(sources, jnp.concatenate([even, odd], axis=0))
        spread.append(
            jnp.concatenate([back[p * 8 : (p + 1) * 8] for p in range(8)], axis=1)
        )
    first_full = exact_pick(pick_second_back[...], jnp.concatenate(spread, axis=0))
    first_grad = jnp.where(real[8:32], first_full * silu_slope(first_pre[8:32]), 0.0).astype(LOW)
    back = across(first_grad, d1_rows[...])
    stacked = jnp.concatenate([back[:, k * 128 : (k + 1) * 128] for k in range(4)], axis=0)
    image_grad = exact_pick(pick_first_back[...], stacked).astype(LOW)
    for part in range(4):
        grads = wide_dot(image_grad, ow_rows[:, part * 1024 : (part + 1) * 1024])
        for c in range(8):
            ag[pl.ds(part * 8 + c, 32, stride=32), :] = grads[:, c * 128 : (c + 1) * 128]

    def weigh(t, acc):
        normed = normed_second(t)
        here = pl.ds(t * 256, 256)
        weighted = ag[here, :] * silu_slope(normed * gain2) * gain2
        ag[here, :] = weighted
        column_copies(t, weighted * inverse2)
        return (
            acc[0] + jnp.sum(weighted, axis=0, keepdims=True),
            acc[1] + jnp.sum(weighted * normed, axis=0, keepdims=True),
        )

    zeros = (jnp.zeros((1, 128), WIDE), jnp.zeros((1, 128), WIDE))
    sums = lax.fori_loop(0, 4, weigh, zeros)
    stats_start(2, *sums)
    against_acts(dw)
    for i in range(9):
        for c in range(3):
            first = (i * 3 + c) * 128
            sums_wide[first : first + 128, :] = jnp.broadcast_to(reach[i, :, c : c + 1], (128, 128))
    for array in (dw, p1, sums_wide):
        array[3456:3520, :] = jnp.zeros((64, 128), WIDE)
    first_mean, second_mean = sums_end(2)

    first_part, second_part = (first_mean * inverse2, second_mean * inverse2)
    theirs = pl.ds(pl.multiple_of((1 - core) * 1728, 64), 1792)
    ours = pl.ds(pl.multiple_of(core * 1728, 64), 1792)
    chunks = (pl.ds(0, 64), pl.ds(64, 48))

    def corrected(rows):
        return dw[rows, :] - sums_wide[rows, :] * first_part - p1[rows, :] * second_part

    pair_out[...] = corrected(theirs).astype(LOW).reshape(16, 112, 128)
    for turn, chunk in enumerate(chunks):
        push(pair_out.at[:, chunk], pair_in.at[:, chunk], partner, sum_send.at[turn], sum_recv.at[turn])

    @pl.loop(0, 4)
    def _(t):
        here = pl.ds(t * 256, 256)
        grad = (ag[here, :] - first_mean - normed_second(t) * second_mean) * inverse2
        ag[here, :] = grad
        ge[t, 1:9] = grad.astype(LOW).reshape(8, 32, 128)

    halo_start(1, ge, ge, 1, (0, 0, 0), 4, -1)

    dw[ours, :] = corrected(ours)
    for turn, chunk in enumerate(chunks):
        arrived(pair_in.at[:, chunk], sum_recv.at[turn])
        mine = dw[ours, :].reshape(16, 112, 128)[:, chunk.start : chunk.start + chunk.size]
        plane_out[:, chunk] = (mine + pair_in[:, chunk].astype(WIDE)).astype(LOW)
        for other, peer in plane_line:
            push(
                plane_out.at[other, chunk],
                plane_in.at[slot, chunk],
                peer,
                sum_send.at[2 + turn],
                sum_recv.at[2 + turn],
            )
        plane_in[slot, chunk] = plane_out[slot, chunk]

    tiles = (range(0, 4), range(4, 7))
    own_tile = z % 8
    owns = (own_tile < 4, (own_tile >= 4) & (own_tile < 7))
    for turn, chunk in enumerate(chunks):
        others = plane_in.at[pl.ds(0, 15), chunk]
        arrived(others, sum_recv.at[2 + turn])
        total = jnp.sum(plane_in[:, chunk].astype(WIDE), axis=0).astype(LOW)
        for index, part in enumerate(tiles[turn]):
            z_out[part] = total[index * 16 : (index + 1) * 16]
            for owner in (part, part + 8):

                @pl.when(z != owner)
                def _():
                    push(
                        z_out.at[part],
                        z_in.at[z],
                        device(me, z_hi=owner // 4, z_lo=owner % 4),
                        sum_send.at[4 + turn],
                        sum_recv.at[4],
                    )

    halo_wait(1, ge, 0, 4)

    def normed_first(t):
        return (own_input(t) - mean1) * inverse1

    def back_step(t, acc):
        taps = []
        for i in range(3):
            for j in range(3):
                strip = ge[t + 2 - i, 2 - j : 10 - j].reshape(256, 128)
                above_edge = (row == 0) if j == 2 else False
                below_edge = (row == 15) if j == 0 else False
                late = (frame == 3) & (t + 2 - i > 3)
                position = lax.broadcasted_iota(jnp.int32, (256, 128), 0)
                low = jnp.where(above_edge, 32, 0)
                end = jnp.where(late, 0, jnp.where(below_edge, 224, 256))
                keep = (position >= low) & (position < end)
                taps.append(jnp.where(keep, strip.astype(WIDE), 0.0).astype(LOW))
        product = wide_dot(jnp.concatenate(taps, axis=1), w_back[...])
        grad = column_sum(product[:, 256:384], product[:, 128:256], product[:, 0:128])
        normed = normed_first(t)
        weighted = grad * silu_slope(normed * gain1) * gain1
        wg[t] = weighted
        return (
            acc[0] + jnp.sum(weighted, axis=0, keepdims=True),
            acc[1] + jnp.sum(weighted * normed, axis=0, keepdims=True),
        )

    sums = lax.fori_loop(0, 4, back_step, zeros)
    plane_start(*sums)

    for turn in range(2):

        @pl.when(owns[turn])
        def _():
            z_in[z] = z_out[own_tile]
            arrived(z_in.at[pl.ds(0, 15)], sum_recv.at[4])
            z_all[own_tile] = jnp.sum(z_in[...].astype(WIDE), axis=0).astype(LOW)
            mine = z_all.at[own_tile]
            for step in (-4, 3, -3, 2, -2, 1, -1):
                other = (z + step) % 16
                peer = device(me, z_hi=other // 4, z_lo=other % 4)
                push(mine, mine, peer, sum_send.at[6], sum_recv.at[6 + turn])

    plane_to_high()

    half, other_half = (gathered.at[core], gathered.at[1 - core])
    for turn, chunk in enumerate(chunks):
        count = len(tiles[turn])

        @pl.when(owns[turn])
        def _():
            arrived(z_all.at[pl.ds(0, count - 1)], sum_recv.at[6 + turn])

        @pl.when(jnp.logical_not(owns[turn]))
        def _():
            arrived(z_all.at[pl.ds(0, count)], sum_recv.at[6 + turn])

        first = tiles[turn].start
        half[slot, chunk] = z_all[first : first + count].reshape(count * 16, 128)
        for _, peer in plane_line:
            push(
                half.at[slot, chunk],
                half.at[slot, chunk],
                peer,
                sum_send.at[8 + turn],
                sum_recv.at[8 + turn],
            )

    first_mean, second_mean = high_end()

    @pl.loop(0, 4)
    def _(t):
        grad = (wg[t] - first_mean - normed_first(t) * second_mean) * inverse1
        out_ref[t] = (ag[pl.ds(t * 256, 256), :] + grad).astype(LOW).reshape(8, 32, 128)

    out_copy = pltpu.make_async_copy(out_ref, grad_hbm, load_sem.at[12])
    out_copy.start()

    def squares_of(part_of, chunk):
        def add(part, acc):
            piece = part_of[part, chunk].astype(WIDE)
            return acc + jnp.sum((piece * piece).reshape(chunk.size // 8, 8, 128), axis=0)

        total = lax.fori_loop(0, 15, add, jnp.zeros((8, 128), WIDE))
        if chunk.start == 0:
            piece = part_of[15, 0:48].astype(WIDE)
            total = total + jnp.sum((piece * piece).reshape(6, 8, 128), axis=0)
        return total

    squares = []
    for turn, chunk in enumerate(chunks):
        others = half.at[pl.ds(0, 15), chunk]
        arrived(others, sum_recv.at[8 + turn])
        push(half.at[:, chunk], half.at[:, chunk], partner, sum_send.at[10 + turn], sum_recv.at[10 + turn])
        squares.append(squares_of(half, chunk))
    own_copy = pltpu.make_async_copy(half, summed_hbm.at[core], load_sem.at[13])
    own_copy.start()
    other_copies = []
    for turn, chunk in enumerate(chunks):
        arrived(other_half.at[:, chunk], sum_recv.at[10 + turn])
        other_copies.append(
            pltpu.make_async_copy(
                other_half.at[:, chunk], summed_hbm.at[1 - core, :, chunk], load_sem.at[14 + turn]
            )
        )
        other_copies[-1].start()
        squares.append(squares_of(other_half, chunk))
    total = (squares[0] + squares[1]) + (squares[2] + squares[3])
    mean = jnp.sum(total, keepdims=True) / (3456.0 * 128.0)
    scale_ref[...] = jnp.broadcast_to(lax.rsqrt(mean + EPSILON), (8, 128))

    for turn in range(3):
        arrived(stats.at[turn, pl.ds(0, 63)], stat_send.at[turn])
    arrived(plane.at[pl.ds(0, 15)], stat_send.at[3])
    arrived(high.at[pl.ds(0, 3)], stat_send.at[4])
    for turn, chunk in enumerate(chunks):
        count = len(tiles[turn])
        arrived(pair_in.at[:, chunk], sum_send.at[turn])
        arrived(plane_in.at[pl.ds(0, 15), chunk], sum_send.at[2 + turn])
        arrived(half.at[pl.ds(0, 15), chunk], sum_send.at[8 + turn])
        arrived(half.at[:, chunk], sum_send.at[10 + turn])

        @pl.when(owns[turn])
        def _():
            arrived(z_in.at[pl.ds(0, 2 * count - 1)], sum_send.at[4 + turn])
            arrived(z_in.at[pl.ds(0, 7)], sum_send.at[6])

        @pl.when(jnp.logical_not(owns[turn]))
        def _():
            arrived(z_in.at[pl.ds(0, 2 * count)], sum_send.at[4 + turn])

    for copy in [out_copy, own_copy] + other_copies:
        copy.wait()


def finish_kernel(grad_ref, summed_ref, scale_ref, out_ref, upd_ref):
    out_ref[...] = grad_ref[...]
    scale = scale_ref[0:1, :]
    values = summed_ref[0, 0:15].reshape(1680, 128)
    upd_ref[0, 0:1680, :] = values.astype(WIDE) * scale
    upd_ref[0, 1680:1728, :] = summed_ref[0, 15, 0:48].astype(WIDE) * scale


def shards(
    block_input, gain_first, conv_weight, gain_second, out_weight, disc_first, disc_second, score_grad
):
    vmem = pl.BlockSpec(memory_space=pltpu.VMEM)
    low = lambda *shape: pltpu.VMEM(shape, LOW)
    wide = lambda *shape: pltpu.VMEM(shape, WIDE)
    dma = pltpu.SemaphoreType.DMA
    picks = selections()
    hbm = pl.BlockSpec(memory_space=pltpu.HBM)
    input_grad, summed, scale = pl.pallas_call(
        step_kernel,
        out_shape=(
            jax.ShapeDtypeStruct((4, 8, 32, 128), LOW),
            jax.ShapeDtypeStruct((2, 16, 112, 128), LOW),
            jax.ShapeDtypeStruct((8, 128), WIDE),
        ),
        in_specs=[hbm] * 12,
        out_specs=(hbm, hbm, vmem),
        scratch_shapes=[
            low(4, 8, 32, 128), wide(1, 128), low(27, 128, 128), wide(1, 128), low(3, 128), low(12, 4, 64),
            low(32, 64, 128), low(160, 96), low(64, 40), wide(24, 64), wide(32, 96),
            low(6, 10, 32, 128), low(6, 10, 32, 128), low(6, 10, 32, 128),
            low(4, 256, 128), wide(1024, 128), wide(4, 256, 128),
            low(3, 6, 128, 256), low(1024, 384), low(1152, 384), low(1152, 384),
            wide(128, 128), low(4096, 128), low(128, 4096), wide(128, 128), low(512, 1024),
            low(3, 32, 128), wide(2, 4, 8, 128), wide(64, 128),
            wide(3520, 128), wide(3520, 128), wide(9, 128, 128), wide(3520, 128), low(16, 112, 128), low(16, 112, 128), low(16, 112, 128), low(16, 112, 128),
            low(7, 16, 128), low(16, 16, 128), low(7, 16, 128), low(2, 16, 112, 128),
            wide(3, 64, 2, 128), wide(16, 2, 128), wide(4, 2, 128),
            dma((16,)), dma((5,)), dma((5,)), dma((2, 7)), dma((2, 7)), dma((12,)), dma((12,)),
        ],
        compiler_params=pltpu.CompilerParams(
            collective_id=1, has_side_effects=True, vmem_limit_bytes=64 * 1024 * 1024
        ),
    )(
        block_input[0],
        gain_first.reshape(1, 128),
        conv_weight.reshape(27, 128, 128),
        gain_second.reshape(1, 128),
        out_weight.T,
        disc_first[0].transpose(0, 2, 1, 3).reshape(12, 4, 64),
        disc_second.reshape(32, 64, 128),
        score_grad[0],
        *picks,
    )
    input_grad, update = pl.pallas_call(
        finish_kernel,
        out_shape=(
            jax.ShapeDtypeStruct((4, 8, 32, 128), LOW),
            jax.ShapeDtypeStruct((2, 1728, 128), WIDE),
        ),
        grid=(2,),
        in_specs=[
            pl.BlockSpec((2, 8, 32, 128), lambda half: (half, 0, 0, 0)),
            pl.BlockSpec((1, 16, 112, 128), lambda half: (half, 0, 0, 0)),
            pl.BlockSpec((8, 128), lambda half: (0, 0)),
        ],
        out_specs=(
            pl.BlockSpec((2, 8, 32, 128), lambda half: (half, 0, 0, 0)),
            pl.BlockSpec((1, 1728, 128), lambda half: (half, 0, 0)),
        ),
        compiler_params=pltpu.CompilerParams(vmem_limit_bytes=64 * 1024 * 1024),
    )(input_grad, summed, scale)
    return (input_grad[None], update.reshape(conv_weight.shape))


def solution(mesh):
    split = P("batch", "frame", "row", None, None)
    in_specs = (split, P(), P(), P(), P(), P(), P(), split)
    return jax.shard_map(
        shards, mesh=mesh, in_specs=in_specs, out_specs=(split, P()), check_vma=False
    )
```
